256 devices in a mesh: seq: 16 (over y_hi, z), inner: 8 (over x, core), chan: 2 (over y_lo).
Axes of the slice: x: 4, y: 4 (y_hi: 2, y_lo: 2; y = y_hi * 2 + y_lo), z: 8, core: 2. Of those that a mesh axis runs over, the one named last changes fastest.
Arguments:
- gate_query: bfloat16 [16384, 512], P(('seq', 'inner'), 'chan'), may hold values from -6 to 6
- gate_key: bfloat16 [16384, 512], P(('seq', 'inner'), 'chan'), may hold values from -6 to 6
- value_input: bfloat16 [16384, 512], P(('seq', 'inner'), 'chan'), may hold values from -6 to 6
- filter_taps: bfloat16 [32, 16384], P('chan', ('seq', 'inner')), may hold values from -4 to 4
- grad_output: bfloat16 [16384, 512], P(('seq', 'inner'), 'chan'), may hold values from -1.5 to 1.5
Outputs:
- mixed_out: bfloat16 [16384, 512], P(('seq', 'inner'), 'chan')
- grad_query: bfloat16 [16384, 512], P(('seq', 'inner'), 'chan')
- grad_key: bfloat16 [16384, 512], P(('seq', 'inner'), 'chan')
- grad_value: bfloat16 [16384, 512], P(('seq', 'inner'), 'chan')
- grad_filter: float32 [32, 16384], P('chan', ('seq', 'inner'))
The draws below stay inside these ranges and needn't reach their ends.
All inputs are finite; a program needn't handle non-finite values.
Results may differ from the reference program's by a relative error of at most 0.0007.
Values may be sent and summed in bfloat16 or wider, within the bound.
No kernel may reach another device: no remote copies, remote signals or barrier semaphores. Data moves between devices by JAX's collectives and lax.ppermute only.
A program may use at most 64 MiB of HBM per device.

```python
import math
import jax
import jax.numpy as jnp
from jax import lax

GROUP_CH = 16
GROUPS = 32
CH = 512
SEQ = 16384


def draw_filter_taps(key, part):
    key = jax.random.fold_in(key, 17)
    rough_part = jnp.clip(jax.random.normal(key, (GROUPS, SEQ), jnp.float32), -4.0, 4.0)
    return rough_part.astype(jnp.bfloat16)


def level_of(own_key, dims, cuts, least, largest):
    factor_of, own = 1.0, jax.random.fold_in(own_key, 6)
    for position, shards_of in cuts:
        draws = jnp.exp(jax.random.uniform(jax.random.fold_in(own, position), (shards_of,), jnp.float32, least / len(cuts), largest / len(cuts)))
        factor_of = factor_of * jnp.repeat(draws, dims[position] // shards_of).reshape([-1 if axis == position else 1 for axis in range(len(dims))])
    return factor_of


def normal_values(own_key, shape, deviation, reach, shards=(), kind=jnp.bfloat16):
    drawn = jax.random.normal(own_key, shape, jnp.float32) * deviation
    if len(shards) > 0:
        drawn = level_of(own_key, shape, shards, -0.22, 0.18) * drawn
    return jnp.clip(drawn, min=-reach, max=reach).astype(kind)


def setup_inputs(seed: int = 0) -> dict:
    keys = jax.random.split(jax.random.key(seed), 6)
    gate_query = normal_values(keys[0], (SEQ, CH), 1.0, 6.0, ((0, 128), (1, 2)))
    gate_key = normal_values(keys[1], (SEQ, CH), 1.0, 6.0, ((0, 128), (1, 2)))
    value_input = normal_values(keys[2], (SEQ, CH), 1.0, 6.0, ((0, 128), (1, 2)))
    filter_taps = draw_filter_taps(jax.random.fold_in(keys[5], 71), 0)
    grad_output = normal_values(keys[4], (SEQ, CH), 0.25, 1.5, ((0, 128), (1, 2)))
    return {"gate_query": gate_query, "gate_key": gate_key, "value_input": value_input, "filter_taps": filter_taps, "grad_output": grad_output}


def channel_block(pieces, factor):
    query_block, key_block, value_block, upstream_block, taps_block = pieces
    length = query_block.shape[0]
    padded = 2 * length
    taps_channels = jnp.repeat(jnp.transpose(taps_block), GROUP_CH, axis=1)
    position_product = key_block.astype(jnp.float32) * value_block.astype(jnp.float32)
    value_spectrum = jnp.fft.rfft(position_product, n=padded, axis=0)
    causal = jnp.fft.irfft(value_spectrum * taps_channels, n=padded, axis=0)[:length] * factor
    query_values = query_block.astype(jnp.float32)
    upstream_values = upstream_block.astype(jnp.float32)
    mixed_out = (query_values * causal).astype(jnp.bfloat16)
    grad_query = (upstream_values * causal).astype(jnp.bfloat16)
    gated_grad = upstream_values * query_values
    grad_spectrum = jnp.fft.rfft(gated_grad, n=padded, axis=0)
    back_conv = jnp.fft.irfft(jnp.conj(taps_channels) * grad_spectrum, n=padded, axis=0)[:length] * factor
    grad_key = (back_conv * value_block.astype(jnp.float32)).astype(jnp.bfloat16)
    grad_value = (back_conv * key_block.astype(jnp.float32)).astype(jnp.bfloat16)
    cross_full = jnp.conj(value_spectrum) * grad_spectrum
    cross_term = lax.optimization_barrier(jnp.sum(cross_full.reshape(cross_full.shape[0], -1, GROUP_CH), axis=2))
    return (mixed_out, grad_query, grad_key, grad_value, jnp.real(cross_term), jnp.imag(cross_term))

def reference(gate_query, gate_key, value_input, filter_taps, grad_output):
    length, channels = gate_query.shape
    block_width = 64 if channels % 64 == 0 else channels
    block_count = channels // block_width
    group_total = channels // GROUP_CH
    groups_block = block_width // GROUP_CH
    factor = 1.0 / math.sqrt(length)
    taps_spectrum = jnp.fft.rfft(filter_taps.astype(jnp.float32), n=2 * length, axis=1)
    taps_blocks = taps_spectrum.reshape(block_count, groups_block, length + 1)

    def split_blocks(source):
        return source.reshape(length, block_count, block_width).transpose(1, 0, 2)

    def join_blocks(source):
        return source.transpose(1, 0, 2).reshape(length, channels)

    def run_block(pieces):
        return channel_block(pieces, factor)
    results = lax.map(run_block, (split_blocks(gate_query), split_blocks(gate_key), split_blocks(value_input), split_blocks(grad_output), taps_blocks))
    cross_real = results[4].transpose(0, 2, 1).reshape(group_total, length + 1)
    cross_imag = results[5].transpose(0, 2, 1).reshape(group_total, length + 1)
    cross_term = lax.complex(cross_real, cross_imag)
    grad_filter = jnp.fft.irfft(cross_term, n=2 * length, axis=1)[:, :length] * factor
    return (join_blocks(results[0]), join_blocks(results[1]), join_blocks(results[2]), join_blocks(results[3]), grad_filter)
```

```python
import math

import jax
import jax.numpy as jnp
import numpy as np
from jax import lax
from jax.experimental import pallas as pl
from jax.experimental.pallas import tpu as pltpu
from jax.sharding import PartitionSpec as P

AXES = ("seq", "inner")
PIECES = 128
ROWS = 128
CHANNELS = 256
GROUPS = 16
LENGTH = PIECES * ROWS
PADDED = 2 * LENGTH
OUTER = 2 * PIECES
SLOTS = 5
F32 = jnp.float32
BF16 = jnp.bfloat16


def split_table(table):
    high = table.astype(np.float32).astype(jnp.bfloat16)
    low = (table - high.astype(np.float64)).astype(jnp.bfloat16)
    return high, low


def tables():
    k1 = np.arange(OUTER)
    t1 = np.arange(PIECES)
    t2 = np.arange(ROWS)
    outer = np.exp(-2j * np.pi * ((k1[:, None] * t1[None, :]) % OUTER) / OUTER)
    inner = np.exp(-2j * np.pi * ((t2[:, None] * t2[None, :]) % ROWS) / ROWS)
    twist = np.exp(-2j * np.pi * (k1[:, None] * t2[None, :]) / PADDED)
    first = np.concatenate((outer.real, outer.imag), axis=0)
    second = np.block([[inner.real, inner.imag], [-inner.imag, inner.real]])
    scale = 1.0 / (math.sqrt(LENGTH) * PADDED)
    last = np.concatenate((outer.real.T, outer.imag.T), axis=0) * scale
    first_high, first_low = split_table(first)
    second_high, second_low = split_table(second)
    last_high, last_low = split_table(last)
    return (
        np.concatenate((first_high, first_low, first_high), axis=1),
        np.concatenate((second_high, second_high, second_low), axis=0),
        np.stack((twist.real, twist.imag)).astype(np.float32),
        np.concatenate((last_high, last_high, last_low), axis=1),
    )


def split(values):
    high = values.astype(BF16)
    low = (values - high.astype(F32)).astype(BF16)
    return high, low


def dot(left, right):
    return jnp.dot(left, right, preferred_element_type=F32)


def slot(ref, index):
    return ref[pl.ds(index, PIECES, stride=SLOTS), :]


def put_slot(ref, index, values):
    ref[pl.ds(index, PIECES, stride=SLOTS), :] = values


def pack_kernel(query_ref, key_ref, value_ref, taps_ref, upstream_ref, out_ref):
    def place(first, left, right):
        product = left[...].astype(F32) * right[...].astype(F32)
        turned = jnp.transpose(product).reshape(GROUPS, 2, 8, ROWS)
        put_slot(out_ref, first, turned[:, 0].reshape(PIECES, ROWS))
        put_slot(out_ref, first + 1, turned[:, 1].reshape(PIECES, ROWS))

    place(0, key_ref, value_ref)
    place(2, upstream_ref, query_ref)
    taps = taps_ref[...].astype(F32)
    spread = jnp.broadcast_to(taps[:, None, :], (GROUPS, 8, ROWS)).reshape(PIECES, ROWS)
    put_slot(out_ref, 4, spread)


def convolve_kernel(in_ref, first_ref, second_ref, twist_ref, last_ref, out_ref):
    whole = jnp.concatenate([slot(in_ref, i) for i in range(SLOTS)], axis=1)
    high, low = split(whole)
    mixed = dot(first_ref[...], jnp.concatenate((high, high, low), axis=0))
    twist_real, twist_imag = twist_ref[0], twist_ref[1]

    def part(half, index):
        return mixed[half * OUTER : (half + 1) * OUTER, index * ROWS : (index + 1) * ROWS]

    def rotate(real, imag, sign):
        return (
            real * twist_real - sign * (imag * twist_imag),
            imag * twist_real + sign * (real * twist_imag),
        )

    def pair(index):
        return (
            part(0, index) - part(1, index + 1),
            part(1, index) + part(0, index + 1),
        )

    def inner(real, imag):
        high, low = split(jnp.concatenate((real, imag), axis=1))
        result = dot(jnp.concatenate((high, low, high), axis=1), second_ref[...])
        return result[:, :ROWS], result[:, ROWS:]

    value_real, value_imag = inner(*rotate(*pair(0), 1.0))
    grad_real, grad_imag = inner(*rotate(*pair(2), 1.0))
    taps_real, taps_imag = inner(*rotate(part(0, 4), part(1, 4), 1.0))

    def back(real, imag):
        turned_imag, turned_real = inner(imag, real)
        return jnp.concatenate(rotate(turned_real, turned_imag, -1.0), axis=1)

    spectra = jnp.concatenate(
        (
            back(
                value_real * taps_real - value_imag * taps_imag,
                value_real * taps_imag + value_imag * taps_real,
            ),
            back(
                grad_real * taps_real + grad_imag * taps_imag,
                grad_imag * taps_real - grad_real * taps_imag,
            ),
            back(
                grad_real * value_real + grad_imag * value_imag,
                grad_imag * value_real - grad_real * value_imag,
            ),
        ),
        axis=1,
    )
    high, low = split(spectra)
    final = dot(last_ref[...], jnp.concatenate((high, low, high), axis=0))

    def block(half, index):
        return final[half * PIECES : (half + 1) * PIECES, index * ROWS : (index + 1) * ROWS]

    put_slot(out_ref, 0, block(0, 0) + block(1, 1))
    put_slot(out_ref, 1, block(0, 1) - block(1, 0))
    put_slot(out_ref, 2, block(0, 2) + block(1, 3))
    put_slot(out_ref, 3, block(0, 3) - block(1, 2))
    put_slot(out_ref, 4, block(0, 4) + block(1, 5))


def finish_kernel(
    in_ref, query_ref, key_ref, value_ref, upstream_ref, mixed_ref, gquery_ref, gkey_ref, gvalue_ref, gfilter_ref
):
    def collect(first):
        one = slot(in_ref, first).reshape(GROUPS, 1, 8, ROWS)
        two = slot(in_ref, first + 1).reshape(GROUPS, 1, 8, ROWS)
        return jnp.transpose(jnp.concatenate((one, two), axis=1).reshape(CHANNELS, ROWS))

    causal = collect(0)
    mixed_ref[...] = (query_ref[...].astype(F32) * causal).astype(BF16)
    gquery_ref[...] = (upstream_ref[...].astype(F32) * causal).astype(BF16)
    back_conv = collect(2)
    gkey_ref[...] = (back_conv * value_ref[...].astype(F32)).astype(BF16)
    gvalue_ref[...] = (back_conv * key_ref[...].astype(F32)).astype(BF16)
    gfilter_ref[...] = jnp.sum(slot(in_ref, 4).reshape(GROUPS, 8, ROWS), axis=1)


def exchange(blocks):
    return lax.all_to_all(
        blocks.reshape(PIECES * SLOTS, 1, ROWS), AXES, split_axis=0, concat_axis=0, tiled=True
    ).reshape(PIECES * SLOTS, ROWS)


def per_device(gate_query, gate_key, value_input, filter_taps, grad_output):
    packed = jax.ShapeDtypeStruct((PIECES * SLOTS, ROWS), F32)
    blocks = pl.pallas_call(pack_kernel, out_shape=packed)(
        gate_query, gate_key, value_input, filter_taps, grad_output
    )
    received = exchange(blocks)
    results = pl.pallas_call(
        convolve_kernel,
        out_shape=packed,
        compiler_params=pltpu.CompilerParams(vmem_limit_bytes=48 * 1024 * 1024),
    )(received, *(jnp.asarray(table) for table in tables()))
    returned = exchange(results)
    wide = jax.ShapeDtypeStruct((ROWS, CHANNELS), BF16)
    return pl.pallas_call(
        finish_kernel,
        out_shape=(wide, wide, wide, wide, jax.ShapeDtypeStruct((GROUPS, ROWS), F32)),
    )(returned, gate_query, gate_key, value_input, grad_output)


def solution(mesh):
    rows = P(AXES, "chan")
    taps = P("chan", AXES)
    return jax.shard_map(
        per_device,
        mesh=mesh,
        in_specs=(rows, rows, rows, taps, rows),
        out_specs=(rows, rows, rows, rows, taps),
        check_vma=False,
    )
```

```python
import math

import jax
import jax.numpy as jnp
import numpy as np
from jax import lax
from jax.experimental import pallas as pl
from jax.experimental.pallas import tpu as pltpu
from jax.sharding import PartitionSpec as P

AXES = ("seq", "inner")
PIECES = 128
CHIPS = PIECES // 2
ROWS = 128
CHANNELS = 256
GROUPS = 16
SUBS = CHIPS // GROUPS
OWNED = 4
LENGTH = PIECES * ROWS
PADDED = 2 * LENGTH
OUTER = 2 * PIECES
SLOTS = 2 * OWNED + 1
SMALL = 4 * 1024 * 1024
LARGE = 24 * 1024 * 1024
F32 = jnp.float32
BF16 = jnp.bfloat16


def split_table(table):
    high = table.astype(np.float32).astype(jnp.bfloat16)
    low = (table - high.astype(np.float64)).astype(jnp.bfloat16)
    return high, low


def tables():
    k1 = np.arange(OUTER)
    t1 = np.stack((np.arange(0, PIECES, 2), np.arange(1, PIECES, 2)))
    t2 = np.arange(ROWS)
    outer = np.exp(-2j * np.pi * ((k1[None, :, None] * t1[:, None, :]) % OUTER) / OUTER)
    inner = np.exp(-2j * np.pi * ((t2[:, None] * t2[None, :]) % ROWS) / ROWS)
    twist = np.exp(-2j * np.pi * (k1[:, None] * t2[None, :]) / PADDED)
    first = np.concatenate((outer.real, outer.imag), axis=1)
    second = np.block([[inner.real, inner.imag], [-inner.imag, inner.real]])
    scale = 1.0 / (math.sqrt(LENGTH) * PADDED)
    last = np.swapaxes(np.concatenate((outer.real, outer.imag), axis=2), 1, 2) * scale
    first_high, first_low = split_table(first)
    second_high, second_low = split_table(second)
    last_high, last_low = split_table(last)
    return (
        np.concatenate((first_high, first_low, first_high), axis=2),
        np.concatenate((second_high, second_low), axis=0),
        np.stack((twist.real, twist.imag)).astype(np.float32),
        np.concatenate((last_high, last_low), axis=2),
    )


def split(values):
    high = values.astype(BF16)
    low = (values - high.astype(F32)).astype(BF16)
    return high, low


def dot(left, right):
    return jnp.dot(left, right, preferred_element_type=F32)


def chip_rows(slot, first=0, count=CHIPS, slots=SLOTS):
    return pl.ds(first * slots + slot, count, stride=slots)


def slot_of(array, owned):
    return 4 * (owned // 2) + 2 * array + owned % 2


def pack_kernel(
    query_ref, key_ref, value_ref, taps_ref, upstream_ref, out_ref, query, key, value, taps, upstream, turned, sems
):
    moves = (
        (key_ref, key),
        (value_ref, value),
        (upstream_ref, upstream),
        (query_ref, query),
        (taps_ref, taps),
    )
    copies = [pltpu.make_async_copy(a, b, sems.at[i]) for i, (a, b) in enumerate(moves)]
    for copy in copies:
        copy.start()

    def place(array, left, right):
        turned[array] = jnp.transpose(left[...].astype(F32) * right[...].astype(F32))
        for owned in range(OWNED):
            for sub in range(SUBS):
                out_ref[chip_rows(slot_of(array, owned), GROUPS * sub, GROUPS), :] = turned[
                    array, pl.ds(SUBS * owned + sub, GROUPS, stride=GROUPS), :
                ]

    copies[0].wait()
    copies[1].wait()
    place(0, key, value)
    copies[2].wait()
    copies[3].wait()
    place(1, upstream, query)
    copies[4].wait()
    for sub in range(SUBS):
        out_ref[chip_rows(SLOTS - 1, GROUPS * sub, GROUPS), :] = taps[...].astype(F32)


def outer_forward(in_ref, table):
    whole = jnp.concatenate([in_ref[chip_rows(i), :] for i in range(SLOTS)], axis=1)
    high, low = split(whole)
    return dot(table, jnp.concatenate((high, high, low), axis=0))


def own_kernel(core_ref, in_ref, first_ref, out_ref):
    out_ref[...] = outer_forward(in_ref, first_ref[core_ref[0]])


def convolve_kernel(core_ref, other_ref, mixed_ref, first_ref, second_ref, twist_ref, last_ref, out_ref):
    core = core_ref[0]
    mixed = mixed_ref[...] + outer_forward(other_ref, first_ref[1 - core])
    second = jnp.concatenate(
        (second_ref[: 2 * ROWS], second_ref[: 2 * ROWS], second_ref[2 * ROWS :]), axis=0
    )
    twist_real, twist_imag = twist_ref[0], twist_ref[1]

    def part(half, index):
        return mixed[half * OUTER : (half + 1) * OUTER, index * ROWS : (index + 1) * ROWS]

    def rotate(real, imag, sign):
        return (
            real * twist_real - sign * (imag * twist_imag),
            imag * twist_real + sign * (real * twist_imag),
        )

    def inner(real, imag):
        high, low = split(jnp.concatenate((real, imag), axis=1))
        result = dot(jnp.concatenate((high, low, high), axis=1), second)
        return result[:, :ROWS], result[:, ROWS:]

    def forward(slot):
        return inner(
            *rotate(part(0, slot) - part(1, slot + 1), part(1, slot) + part(0, slot + 1), 1.0)
        )

    def back(real, imag):
        turned_imag, turned_real = inner(imag, real)
        return jnp.concatenate(rotate(turned_real, turned_imag, -1.0), axis=1)

    taps_real, taps_imag = inner(*rotate(part(0, SLOTS - 1), part(1, SLOTS - 1), 1.0))
    spectra = []
    cross_real = cross_imag = None
    for pair in range(2):
        value_real, value_imag = forward(4 * pair)
        spectra.append(
            back(
                value_real * taps_real - value_imag * taps_imag,
                value_real * taps_imag + value_imag * taps_real,
            )
        )
        grad_real, grad_imag = forward(4 * pair + 2)
        spectra.append(
            back(
                grad_real * taps_real + grad_imag * taps_imag,
                grad_imag * taps_real - grad_real * taps_imag,
            )
        )
        term_real = grad_real * value_real + grad_imag * value_imag
        term_imag = grad_imag * value_real - grad_real * value_imag
        cross_real = term_real if cross_real is None else cross_real + term_real
        cross_imag = term_imag if cross_imag is None else cross_imag + term_imag
    spectra.append(back(cross_real, cross_imag))
    high, low = split(jnp.concatenate(spectra, axis=1))
    table = last_ref[core]
    last = jnp.concatenate((table[:, :OUTER], table[:, :OUTER], table[:, OUTER:]), axis=1)
    final = dot(last, jnp.concatenate((high, low, high), axis=0))

    def block(half, index):
        return final[half * CHIPS : (half + 1) * CHIPS, index * ROWS : (index + 1) * ROWS]

    for index in range(0, 2 * OWNED, 2):
        out_ref[chip_rows(index), :] = block(0, index) + block(1, index + 1)
        out_ref[chip_rows(index + 1), :] = block(0, index + 1) - block(1, index)
    out_ref[chip_rows(SLOTS - 1), :] = block(0, SLOTS - 1) + block(1, SLOTS)


def finish_kernel(
    in_ref, query_ref, key_ref, value_ref, upstream_ref, mixed_ref, gquery_ref, gkey_ref, gvalue_ref, gfilter_ref, turned
):
    def collect(array):
        for owned in range(OWNED):
            for sub in range(SUBS):
                turned[array, pl.ds(SUBS * owned + sub, GROUPS, stride=GROUPS), :] = in_ref[
                    chip_rows(slot_of(array, owned), GROUPS * sub, GROUPS), :
                ]
        return jnp.transpose(turned[array])

    causal = collect(0)
    mixed_ref[...] = (query_ref[...].astype(F32) * causal).astype(BF16)
    gquery_ref[...] = (upstream_ref[...].astype(F32) * causal).astype(BF16)
    back_conv = collect(1)
    gkey_ref[...] = (back_conv * value_ref[...].astype(F32)).astype(BF16)
    gvalue_ref[...] = (back_conv * key_ref[...].astype(F32)).astype(BF16)
    parts = [in_ref[chip_rows(SLOTS - 1, GROUPS * sub, GROUPS), :] for sub in range(SUBS)]
    gfilter_ref[...] = (parts[0] + parts[1]) + (parts[2] + parts[3])


def swap_cores(values):
    count = lax.axis_size("inner")
    return lax.ppermute(values, "inner", [(i, i ^ 1) for i in range(count)])


def exchange(blocks):
    groups = [list(range(core, PIECES, 2)) for core in range(2)]
    return lax.all_to_all(
        blocks.reshape(CHIPS * SLOTS, 1, ROWS),
        AXES,
        split_axis=0,
        concat_axis=0,
        tiled=True,
        axis_index_groups=groups,
    ).reshape(CHIPS * SLOTS, ROWS)


def per_device(gate_query, gate_key, value_input, filter_taps, grad_output):
    core = (lax.axis_index("inner") % 2).astype(jnp.int32).reshape(1)
    scalar = pl.BlockSpec(memory_space=pltpu.SMEM)
    whole = pl.BlockSpec(memory_space=pltpu.VMEM)
    small = pltpu.CompilerParams(vmem_limit_bytes=SMALL)
    packed = jax.ShapeDtypeStruct((CHIPS * SLOTS, ROWS), F32)
    turned = pltpu.VMEM((2, CHANNELS, ROWS), F32)
    far = pl.BlockSpec(memory_space=pltpu.HBM)
    wide = pltpu.VMEM((ROWS, CHANNELS), BF16)
    sources = (gate_query, gate_key, value_input, filter_taps, grad_output)
    blocks = pl.pallas_call(
        pack_kernel,
        out_shape=packed,
        in_specs=[far] * 5,
        out_specs=whole,
        scratch_shapes=[
            wide,
            wide,
            wide,
            pltpu.VMEM((GROUPS, ROWS), BF16),
            wide,
            turned,
            pltpu.SemaphoreType.DMA((5,)),
        ],
        compiler_params=small,
    )(*(pltpu.with_memory_space_constraint(source, pltpu.HBM) for source in sources))
    received = exchange(blocks)
    other = swap_cores(received)
    first, second, twist, last = (jnp.asarray(table) for table in tables())
    mixed = pl.pallas_call(
        own_kernel,
        out_shape=jax.ShapeDtypeStruct((2 * OUTER, SLOTS * ROWS), F32),
        in_specs=[scalar, whole, whole],
        out_specs=whole,
        compiler_params=pltpu.CompilerParams(vmem_limit_bytes=LARGE),
    )(core, received, first)
    results = pl.pallas_call(
        convolve_kernel,
        out_shape=packed,
        in_specs=[scalar] + [whole] * 6,
        out_specs=whole,
        compiler_params=pltpu.CompilerParams(vmem_limit_bytes=LARGE),
    )(core, other, mixed, first, second, twist, last)
    out = jax.ShapeDtypeStruct((ROWS, CHANNELS), BF16)
    return pl.pallas_call(
        finish_kernel,
        out_shape=(out, out, out, out, jax.ShapeDtypeStruct((GROUPS, ROWS), F32)),
        in_specs=[whole] * 5,
        out_specs=(whole,) * 5,
        scratch_shapes=[turned],
        compiler_params=small,
    )(exchange(results), gate_query, gate_key, value_input, grad_output)


def solution(mesh):
    rows = P(AXES, "chan")
    taps = P("chan", AXES)
    return jax.shard_map(
        per_device,
        mesh=mesh,
        in_specs=(rows, rows, rows, taps, rows),
        out_specs=(rows, rows, rows, rows, taps),
        check_vma=False,
    )
```

```python
import math

import jax
import jax.numpy as jnp
import numpy as np
from jax import lax
from jax.experimental import pallas as pl
from jax.experimental.pallas import tpu as pltpu
from jax.sharding import PartitionSpec as P

AXES = ("seq", "inner")
PIECES = 128
CHIPS = PIECES // 2
ROWS = 128
CHANNELS = 256
GROUPS = 16
SUBS = CHIPS // GROUPS
OWNED = 4
LENGTH = PIECES * ROWS
PADDED = 2 * LENGTH
OUTER = 2 * PIECES
GROUP_SLOT = 2 * OWNED
SCALE_SLOT = GROUP_SLOT + 1
SLOTS = SCALE_SLOT + 1
POWER = 48
RANGE = 125 / POWER
REACH = 2.0 ** (2 * RANGE) - 1.0
SMALL = 4 * 1024 * 1024
LARGE = 24 * 1024 * 1024
F32 = jnp.float32
BF16 = jnp.bfloat16


def split_table(table):
    high = table.astype(np.float32).astype(jnp.bfloat16)
    low = (table - high.astype(np.float64)).astype(jnp.bfloat16)
    return high, low


def tables():
    k1 = np.arange(OUTER)
    k1_half = np.arange(PIECES)
    t1 = np.stack((np.arange(0, PIECES, 2), np.arange(1, PIECES, 2)))
    t2 = np.arange(ROWS)
    outer = np.exp(-2j * np.pi * ((k1_half[None, :, None] * t1[:, None, :]) % OUTER) / OUTER)
    inner = np.exp(-2j * np.pi * ((t2[:, None] * t2[None, :]) % ROWS) / ROWS)
    twist = np.exp(-2j * np.pi * (k1[:, None] * t2[None, :]) / PADDED)
    first = np.concatenate((outer.real, outer.imag), axis=1)
    second = np.block([[inner.real, inner.imag], [-inner.imag, inner.real]])
    scale = 1.0 / (math.sqrt(LENGTH) * PADDED)
    last = np.swapaxes(np.concatenate((outer.real, outer.imag), axis=2), 1, 2) * scale
    first_high, first_low = split_table(first)
    second_high, second_low = split_table(second)
    last_high, last_low = split_table(last)
    return (
        np.concatenate((first_high, first_low, first_high), axis=2),
        np.concatenate((second_high, second_low), axis=0),
        np.stack((twist.real, twist.imag)).astype(np.float32),
        np.concatenate((last_high, last_low), axis=2),
    )


def split(values):
    high = values.astype(BF16)
    low = (values - high.astype(F32)).astype(BF16)
    return high, low


def dot(left, right):
    return jnp.dot(left, right, preferred_element_type=F32)


def scale_of(*arrays):
    peak = jnp.max(jnp.abs(arrays[0]), axis=(0, 1), keepdims=True)
    for array in arrays[1:]:
        peak = jnp.maximum(peak, jnp.max(jnp.abs(array), axis=(0, 1), keepdims=True))
    return (jnp.maximum(peak, 2.0**-118) * 1.0078125).astype(BF16).astype(F32)


def encode(values, scale):
    power = jnp.abs(values) * (REACH * 2.0**-RANGE / scale) + 2.0**-RANGE
    for _ in range(4):
        power = power * power
    power = power * (power * power)
    return jnp.where(values < 0, -power, power)


def decode(codes, scale):
    size = jnp.exp2(jnp.log2(jnp.abs(codes)) * (1.0 / POWER) + RANGE) - 1.0
    size = size * (scale * (1.0 / REACH))
    return jnp.where(codes < 0, -size, size)


def chip_rows(slot, first=0, count=CHIPS):
    return pl.ds(first * SLOTS + slot, count, stride=SLOTS)


def slot_of(array, owned):
    return 4 * (owned // 2) + 2 * array + owned % 2


def pack_kernel(
    query_ref, key_ref, value_ref, taps_ref, upstream_ref, out_ref, query, key, value, taps, upstream, turned, rows, sems
):
    moves = (
        (key_ref, key),
        (value_ref, value),
        (upstream_ref, upstream),
        (query_ref, query),
        (taps_ref, taps),
    )
    copies = [pltpu.make_async_copy(a, b, sems.at[i]) for i, (a, b) in enumerate(moves)]
    for copy in copies:
        copy.start()

    def place(array, left, right):
        product = left[...].astype(F32) * right[...].astype(F32)
        scale = scale_of(product)
        turned[array] = encode(jnp.transpose(product), scale)
        for owned in range(OWNED):
            for sub in range(SUBS):
                rows[chip_rows(slot_of(array, owned), GROUPS * sub, GROUPS), :] = turned[
                    array, pl.ds(SUBS * owned + sub, GROUPS, stride=GROUPS), :
                ]
        return scale

    copies[0].wait()
    copies[1].wait()
    value_scale = place(0, key, value)
    copies[2].wait()
    copies[3].wait()
    grad_scale = place(1, upstream, query)
    copies[4].wait()
    for sub in range(SUBS):
        rows[chip_rows(GROUP_SLOT, GROUPS * sub, GROUPS), :] = taps[...].astype(F32)
    lane = lax.broadcasted_iota(jnp.int32, (CHIPS, ROWS), 1)
    rows[chip_rows(SCALE_SLOT), :] = jnp.where(lane < ROWS // 2, value_scale, grad_scale)
    out_ref[...] = rows[...].astype(BF16)


def outer_forward(in_ref, rows, table):
    rows[...] = in_ref[...].astype(F32)
    scales = rows[chip_rows(SCALE_SLOT), :]
    value_scale, grad_scale = scales[:, :1], scales[:, ROWS // 2 : ROWS // 2 + 1]
    parts = [
        decode(rows[chip_rows(slot), :], grad_scale if slot % 4 > 1 else value_scale)
        for slot in range(GROUP_SLOT)
    ]
    high, low = split(jnp.concatenate(parts + [rows[chip_rows(GROUP_SLOT), :]], axis=1))
    mixed = dot(table, jnp.concatenate((high, high, low), axis=0))

    def part(half, slot):
        return mixed[half * PIECES : (half + 1) * PIECES, slot * ROWS : (slot + 1) * ROWS]

    results = [
        (part(0, slot) - part(1, slot + 1), part(1, slot) + part(0, slot + 1))
        for slot in range(0, 2 * OWNED, 2)
    ]
    return results + [(part(0, GROUP_SLOT), part(1, GROUP_SLOT))]


def own_kernel(core_ref, in_ref, first_ref, out_ref, rows):
    for index, (real, imag) in enumerate(outer_forward(in_ref, rows, first_ref[core_ref[0]])):
        out_ref[:, 2 * index * ROWS : (2 * index + 1) * ROWS] = real
        out_ref[:, (2 * index + 1) * ROWS : (2 * index + 2) * ROWS] = imag


def convolve_kernel(core_ref, other_ref, own_ref, first_ref, second_ref, twist_ref, last_ref, out_ref, rows):
    core = core_ref[0]
    sign = (1 - 2 * core).astype(F32)
    second = jnp.concatenate(
        (second_ref[: 2 * ROWS], second_ref[: 2 * ROWS], second_ref[2 * ROWS :]), axis=0
    )
    table = last_ref[core]
    last = jnp.concatenate((table[:, :PIECES], table[:, :PIECES], table[:, PIECES:]), axis=1)
    twist_real, twist_imag = twist_ref[0], twist_ref[1]

    def rotate(real, imag, sign):
        return (
            real * twist_real - sign * (imag * twist_imag),
            imag * twist_real + sign * (real * twist_imag),
        )

    def inner(real, imag):
        high, low = split(jnp.concatenate((real, imag), axis=1))
        result = dot(jnp.concatenate((high, low, high), axis=1), second)
        return result[:, :ROWS], result[:, ROWS:]

    def both(index, part, other):
        column = (2 * index + part) * ROWS
        own = own_ref[:, column : column + ROWS]
        return jnp.concatenate((own + other, sign * (own - other)), axis=0)

    def forward(index, real, imag):
        return inner(*rotate(both(index, 0, real), both(index, 1, imag), 1.0))

    def back(real, imag):
        turned_imag, turned_real = inner(imag, real)
        turned = jnp.concatenate(rotate(turned_real, turned_imag, -1.0), axis=1)
        return turned[:PIECES] + sign * turned[PIECES:]

    others = outer_forward(other_ref, rows, first_ref[1 - core])
    taps_real, taps_imag = forward(4, *others[4])
    spectra = []
    cross_real = cross_imag = None
    for pair in range(2):
        value_real, value_imag = forward(2 * pair, *others[2 * pair])
        spectra.append(
            back(
                value_real * taps_real - value_imag * taps_imag,
                value_real * taps_imag + value_imag * taps_real,
            )
        )
        grad_real, grad_imag = forward(2 * pair + 1, *others[2 * pair + 1])
        spectra.append(
            back(
                grad_real * taps_real + grad_imag * taps_imag,
                grad_imag * taps_real - grad_real * taps_imag,
            )
        )
        term_real = grad_real * value_real + grad_imag * value_imag
        term_imag = grad_imag * value_real - grad_real * value_imag
        cross_real = term_real if cross_real is None else cross_real + term_real
        cross_imag = term_imag if cross_imag is None else cross_imag + term_imag
    spectra.append(back(cross_real, cross_imag))
    high, low = split(jnp.concatenate(spectra, axis=1))
    final = dot(last, jnp.concatenate((high, low, high), axis=0))

    def block(half, index):
        return final[half * CHIPS : (half + 1) * CHIPS, index * ROWS : (index + 1) * ROWS]

    results = []
    for slot in range(0, GROUP_SLOT, 2):
        results.append(block(0, slot) + block(1, slot + 1))
        results.append(block(0, slot + 1) - block(1, slot))
    gfilter = block(0, GROUP_SLOT) + block(1, GROUP_SLOT + 1)
    causal_scale = scale_of(*(result for slot, result in enumerate(results) if slot % 4 < 2))
    back_scale = scale_of(*(result for slot, result in enumerate(results) if slot % 4 > 1))
    gfilter_scale = scale_of(gfilter)
    for slot, result in enumerate(results):
        rows[chip_rows(slot), :] = encode(result, back_scale if slot % 4 > 1 else causal_scale)
    rows[chip_rows(GROUP_SLOT), :] = encode(gfilter, gfilter_scale)
    lane = lax.broadcasted_iota(jnp.int32, (CHIPS, ROWS), 1)
    rows[chip_rows(SCALE_SLOT), :] = jnp.where(
        lane < ROWS // 4, causal_scale, jnp.where(lane < ROWS // 2, back_scale, gfilter_scale)
    )
    out_ref[...] = rows[...].astype(BF16)


def finish_kernel(
    in_ref,
    query_ref,
    key_ref,
    value_ref,
    upstream_ref,
    mixed_ref,
    gquery_ref,
    gkey_ref,
    gvalue_ref,
    gfilter_ref,
    mixed,
    gquery,
    gkey,
    gvalue,
    gfilter,
    turned,
    rows,
    sems,
):
    copies = []

    def send(source, target):
        copy = pltpu.make_async_copy(source, target, sems.at[len(copies)])
        copy.start()
        copies.append(copy)

    rows[...] = in_ref[...].astype(F32)
    scales = rows[chip_rows(SCALE_SLOT), :]

    def collect(array):
        scale = scales[:, array * ROWS // 4 : array * ROWS // 4 + 1]
        for owned in range(OWNED):
            values = decode(rows[chip_rows(slot_of(array, owned)), :], scale)
            for sub in range(SUBS):
                turned[array, pl.ds(SUBS * owned + sub, GROUPS, stride=GROUPS), :] = values[
                    GROUPS * sub : GROUPS * (sub + 1)
                ]
        return jnp.transpose(turned[array])

    causal = collect(0)
    mixed[...] = (query_ref[...].astype(F32) * causal).astype(BF16)
    send(mixed, mixed_ref)
    gquery[...] = (upstream_ref[...].astype(F32) * causal).astype(BF16)
    send(gquery, gquery_ref)
    back_conv = collect(1)
    gkey[...] = (back_conv * value_ref[...].astype(F32)).astype(BF16)
    send(gkey, gkey_ref)
    gvalue[...] = (back_conv * key_ref[...].astype(F32)).astype(BF16)
    send(gvalue, gvalue_ref)
    shares = decode(rows[chip_rows(GROUP_SLOT), :], scales[:, ROWS // 2 : ROWS // 2 + 1])
    parts = [shares[GROUPS * sub : GROUPS * (sub + 1)] for sub in range(SUBS)]
    gfilter[...] = (parts[0] + parts[1]) + (parts[2] + parts[3])
    send(gfilter, gfilter_ref)
    for copy in copies:
        copy.wait()


def swap_cores(values):
    count = lax.axis_size("inner")
    return lax.ppermute(values, "inner", [(i, i ^ 1) for i in range(count)])


def exchange(blocks):
    groups = [list(range(core, PIECES, 2)) for core in range(2)]
    return lax.all_to_all(
        blocks.reshape(CHIPS * SLOTS // 2, 2, ROWS),
        AXES,
        split_axis=0,
        concat_axis=0,
        tiled=True,
        axis_index_groups=groups,
    ).reshape(CHIPS * SLOTS, ROWS)


def per_device(gate_query, gate_key, value_input, filter_taps, grad_output):
    core = (lax.axis_index("inner") % 2).astype(jnp.int32).reshape(1)
    scalar = pl.BlockSpec(memory_space=pltpu.SMEM)
    whole = pl.BlockSpec(memory_space=pltpu.VMEM)
    small = pltpu.CompilerParams(vmem_limit_bytes=SMALL)
    packed = jax.ShapeDtypeStruct((CHIPS * SLOTS, ROWS), BF16)
    rows = pltpu.VMEM((CHIPS * SLOTS, ROWS), F32)
    turned = pltpu.VMEM((2, CHANNELS, ROWS), F32)
    far = pl.BlockSpec(memory_space=pltpu.HBM)
    wide = pltpu.VMEM((ROWS, CHANNELS), BF16)
    sources = (gate_query, gate_key, value_input, filter_taps, grad_output)
    blocks = pl.pallas_call(
        pack_kernel,
        out_shape=packed,
        in_specs=[far] * 5,
        out_specs=whole,
        scratch_shapes=[
            wide,
            wide,
            wide,
            pltpu.VMEM((GROUPS, ROWS), BF16),
            wide,
            turned,
            rows,
            pltpu.SemaphoreType.DMA((5,)),
        ],
        compiler_params=small,
    )(*(pltpu.with_memory_space_constraint(source, pltpu.HBM) for source in sources))
    received = exchange(blocks)
    other = swap_cores(received)
    first, second, twist, last = (jnp.asarray(table) for table in tables())
    own = pl.pallas_call(
        own_kernel,
        out_shape=jax.ShapeDtypeStruct((PIECES, SLOTS * ROWS), F32),
        in_specs=[scalar, whole, whole],
        out_specs=whole,
        scratch_shapes=[rows],
        compiler_params=pltpu.CompilerParams(vmem_limit_bytes=LARGE),
    )(core, received, first)
    results = pl.pallas_call(
        convolve_kernel,
        out_shape=packed,
        in_specs=[scalar] + [whole] * 6,
        out_specs=whole,
        scratch_shapes=[rows],
        compiler_params=pltpu.CompilerParams(vmem_limit_bytes=LARGE),
    )(core, other, own, first, second, twist, last)
    out = jax.ShapeDtypeStruct((ROWS, CHANNELS), BF16)
    return pl.pallas_call(
        finish_kernel,
        out_shape=(out, out, out, out, jax.ShapeDtypeStruct((GROUPS, ROWS), F32)),
        in_specs=[whole] * 5,
        out_specs=(far,) * 5,
        scratch_shapes=[
            wide,
            wide,
            wide,
            wide,
            pltpu.VMEM((GROUPS, ROWS), F32),
            turned,
            rows,
            pltpu.SemaphoreType.DMA((5,)),
        ],
        compiler_params=small,
    )(exchange(results), gate_query, gate_key, value_input, grad_output)


def solution(mesh):
    rows = P(AXES, "chan")
    taps = P("chan", AXES)
    return jax.shard_map(
        per_device,
        mesh=mesh,
        in_specs=(rows, rows, rows, taps, rows),
        out_specs=(rows, rows, rows, rows, taps),
        check_vma=False,
    )
```

```python
import math

import jax
import jax.numpy as jnp
import numpy as np
from jax import lax
from jax.experimental import pallas as pl
from jax.experimental.pallas import tpu as pltpu
from jax.sharding import PartitionSpec as P

AXES = ("seq", "inner")
PIECES = 128
CHIPS = PIECES // 2
ROWS = 128
CHANNELS = 256
GROUPS = 16
SUBS = CHIPS // GROUPS
OWNED = 4
LENGTH = PIECES * ROWS
PADDED = 2 * LENGTH
OUTER = 2 * PIECES
GROUP_SLOT = 2 * OWNED
SCALE_SLOT = GROUP_SLOT + 1
SLOTS = SCALE_SLOT + 1
POWER = 64
RANGE = 125 / POWER
REACH = 2.0 ** (2 * RANGE) - 1.0
SHARE = 8
SMALL = 4 * 1024 * 1024
LARGE = 24 * 1024 * 1024
F32 = jnp.float32
BF16 = jnp.bfloat16


def split_table(table):
    high = table.astype(np.float32).astype(jnp.bfloat16)
    low = (table - high.astype(np.float64)).astype(jnp.bfloat16)
    return high, low


def tables():
    k1 = np.arange(OUTER)
    k1_half = np.arange(PIECES)
    t1 = np.stack((np.arange(0, PIECES, 2), np.arange(1, PIECES, 2)))
    t2 = np.arange(ROWS)
    outer = np.exp(-2j * np.pi * ((k1_half[None, :, None] * t1[:, None, :]) % OUTER) / OUTER)
    inner = np.exp(-2j * np.pi * ((t2[:, None] * t2[None, :]) % ROWS) / ROWS)
    twist = np.exp(-2j * np.pi * (k1[:, None] * t2[None, :]) / PADDED)
    first = np.concatenate((outer.real, outer.imag), axis=1)
    second = np.block([[inner.real, inner.imag], [-inner.imag, inner.real]])
    scale = 1.0 / (math.sqrt(LENGTH) * PADDED)
    last = np.swapaxes(np.concatenate((outer.real, outer.imag), axis=2), 1, 2) * scale
    first_high, first_low = split_table(first)
    second_high, second_low = split_table(second)
    last_high, last_low = split_table(last)
    return (
        np.concatenate((first_high, first_low, first_high), axis=2),
        np.concatenate((second_high, second_low), axis=0),
        np.stack((twist.real, twist.imag)).astype(np.float32),
        np.concatenate((last_high, last_low), axis=2),
    )


def split(values):
    high = values.astype(BF16)
    low = (values - high.astype(F32)).astype(BF16)
    return high, low


def dot(left, right):
    return jnp.dot(left, right, preferred_element_type=F32)


def scale_of(values):
    peak = jnp.max(jnp.abs(values), axis=1, keepdims=True)
    return (jnp.maximum(peak, 2.0**-118) * 1.0078125).astype(BF16).astype(F32)


def encode(values, scale):
    power = jnp.abs(values) * (REACH * 2.0**-RANGE / scale) + 2.0**-RANGE
    for _ in range(6):
        power = power * power
    return jnp.where(values < 0, -power, power)


def scale_at(scales, slot):
    return scales[:, SHARE * slot : SHARE * slot + 1]


def join_scales(scales):
    lane = lax.broadcasted_iota(jnp.int32, (scales[0].shape[0], ROWS), 1)
    joined = scales[0]
    for slot, scale in enumerate(scales[1:], 1):
        joined = jnp.where(lane < SHARE * slot, joined, scale)
    return joined


def decode(codes, scale):
    size = jnp.exp2(jnp.log2(jnp.abs(codes)) * (1.0 / POWER) + RANGE) - 1.0
    size = size * (scale * (1.0 / REACH))
    return jnp.where(codes < 0, -size, size)


def chip_rows(slot, first=0, count=CHIPS):
    return pl.ds(first * SLOTS + slot, count, stride=SLOTS)


def slot_of(array, owned):
    return 4 * (owned // 2) + 2 * array + owned % 2


def pack_kernel(
    query_ref, key_ref, value_ref, taps_ref, upstream_ref, out_ref, query, key, value, taps, upstream, turned, scaled, rows, sems
):
    moves = (
        (key_ref, key),
        (value_ref, value),
        (upstream_ref, upstream),
        (query_ref, query),
        (taps_ref, taps),
    )
    copies = [pltpu.make_async_copy(a, b, sems.at[i]) for i, (a, b) in enumerate(moves)]
    for copy in copies:
        copy.start()

    def place(array, left, right):
        product = left[...].astype(F32) * right[...].astype(F32)
        values = jnp.transpose(product)
        scale = scale_of(values)
        turned[array] = encode(values, scale)
        scaled[array] = jnp.broadcast_to(scale, (CHANNELS, ROWS))
        for owned in range(OWNED):
            for sub in range(SUBS):
                rows[chip_rows(slot_of(array, owned), GROUPS * sub, GROUPS), :] = turned[
                    array, pl.ds(SUBS * owned + sub, GROUPS, stride=GROUPS), :
                ]

    copies[0].wait()
    copies[1].wait()
    place(0, key, value)
    copies[2].wait()
    copies[3].wait()
    place(1, upstream, query)
    copies[4].wait()
    for sub in range(SUBS):
        rows[chip_rows(GROUP_SLOT, GROUPS * sub, GROUPS), :] = taps[...].astype(F32)
        scales = [None] * GROUP_SLOT
        for array in range(2):
            for owned in range(OWNED):
                scales[slot_of(array, owned)] = scaled[
                    array, pl.ds(SUBS * owned + sub, GROUPS, stride=GROUPS), :
                ]
        rows[chip_rows(SCALE_SLOT, GROUPS * sub, GROUPS), :] = join_scales(scales)
    out_ref[...] = rows[...].astype(BF16)


def outer_forward(in_ref, rows, table):
    rows[...] = in_ref[...].astype(F32)
    scales = rows[chip_rows(SCALE_SLOT), :]
    parts = [
        decode(rows[chip_rows(slot), :], scale_at(scales, slot)) for slot in range(GROUP_SLOT)
    ]
    high, low = split(jnp.concatenate(parts + [rows[chip_rows(GROUP_SLOT), :]], axis=1))
    mixed = dot(table, jnp.concatenate((high, high, low), axis=0))

    def part(half, slot):
        return mixed[half * PIECES : (half + 1) * PIECES, slot * ROWS : (slot + 1) * ROWS]

    results = [
        (part(0, slot) - part(1, slot + 1), part(1, slot) + part(0, slot + 1))
        for slot in range(0, 2 * OWNED, 2)
    ]
    return results + [(part(0, GROUP_SLOT), part(1, GROUP_SLOT))]


def own_kernel(core_ref, in_ref, first_ref, out_ref, rows):
    for index, (real, imag) in enumerate(outer_forward(in_ref, rows, first_ref[core_ref[0]])):
        out_ref[:, 2 * index * ROWS : (2 * index + 1) * ROWS] = real
        out_ref[:, (2 * index + 1) * ROWS : (2 * index + 2) * ROWS] = imag


def convolve_kernel(core_ref, other_ref, own_ref, first_ref, second_ref, twist_ref, last_ref, out_ref, rows):
    core = core_ref[0]
    sign = (1 - 2 * core).astype(F32)
    second = jnp.concatenate(
        (second_ref[: 2 * ROWS], second_ref[: 2 * ROWS], second_ref[2 * ROWS :]), axis=0
    )
    table = last_ref[core]
    last = jnp.concatenate((table[:, :PIECES], table[:, :PIECES], table[:, PIECES:]), axis=1)
    twist_real, twist_imag = twist_ref[0], twist_ref[1]

    def rotate(real, imag, sign):
        return (
            real * twist_real - sign * (imag * twist_imag),
            imag * twist_real + sign * (real * twist_imag),
        )

    def inner(real, imag):
        high, low = split(jnp.concatenate((real, imag), axis=1))
        result = dot(jnp.concatenate((high, low, high), axis=1), second)
        return result[:, :ROWS], result[:, ROWS:]

    def both(index, part, other):
        column = (2 * index + part) * ROWS
        own = own_ref[:, column : column + ROWS]
        return jnp.concatenate((own + other, sign * (own - other)), axis=0)

    def forward(index, real, imag):
        return inner(*rotate(both(index, 0, real), both(index, 1, imag), 1.0))

    def back(real, imag):
        turned_imag, turned_real = inner(imag, real)
        turned = jnp.concatenate(rotate(turned_real, turned_imag, -1.0), axis=1)
        return turned[:PIECES] + sign * turned[PIECES:]

    others = outer_forward(other_ref, rows, first_ref[1 - core])
    taps_real, taps_imag = forward(4, *others[4])
    spectra = []
    cross_real = cross_imag = None
    for pair in range(2):
        value_real, value_imag = forward(2 * pair, *others[2 * pair])
        spectra.append(
            back(
                value_real * taps_real - value_imag * taps_imag,
                value_real * taps_imag + value_imag * taps_real,
            )
        )
        grad_real, grad_imag = forward(2 * pair + 1, *others[2 * pair + 1])
        spectra.append(
            back(
                grad_real * taps_real + grad_imag * taps_imag,
                grad_imag * taps_real - grad_real * taps_imag,
            )
        )
        term_real = grad_real * value_real + grad_imag * value_imag
        term_imag = grad_imag * value_real - grad_real * value_imag
        cross_real = term_real if cross_real is None else cross_real + term_real
        cross_imag = term_imag if cross_imag is None else cross_imag + term_imag
    spectra.append(back(cross_real, cross_imag))
    high, low = split(jnp.concatenate(spectra, axis=1))
    final = dot(last, jnp.concatenate((high, low, high), axis=0))

    def block(half, index):
        return final[half * CHIPS : (half + 1) * CHIPS, index * ROWS : (index + 1) * ROWS]

    results = []
    for slot in range(0, GROUP_SLOT, 2):
        results.append(block(0, slot) + block(1, slot + 1))
        results.append(block(0, slot + 1) - block(1, slot))
    results.append(block(0, GROUP_SLOT) + block(1, GROUP_SLOT + 1))
    scales = [scale_of(result) for result in results]
    for slot, result in enumerate(results):
        rows[chip_rows(slot), :] = encode(result, scales[slot])
    rows[chip_rows(SCALE_SLOT), :] = join_scales(
        [jnp.broadcast_to(scale, (CHIPS, ROWS)) for scale in scales]
    )
    out_ref[...] = rows[...].astype(BF16)


def finish_kernel(
    in_ref,
    query_ref,
    key_ref,
    value_ref,
    upstream_ref,
    mixed_ref,
    gquery_ref,
    gkey_ref,
    gvalue_ref,
    gfilter_ref,
    mixed,
    gquery,
    gkey,
    gvalue,
    gfilter,
    turned,
    rows,
    sems,
):
    copies = []

    def send(source, target):
        copy = pltpu.make_async_copy(source, target, sems.at[len(copies)])
        copy.start()
        copies.append(copy)

    rows[...] = in_ref[...].astype(F32)
    scales = rows[chip_rows(SCALE_SLOT), :]

    def collect(array):
        for owned in range(OWNED):
            slot = slot_of(array, owned)
            values = decode(rows[chip_rows(slot), :], scale_at(scales, slot))
            for sub in range(SUBS):
                turned[array, pl.ds(SUBS * owned + sub, GROUPS, stride=GROUPS), :] = values[
                    GROUPS * sub : GROUPS * (sub + 1)
                ]
        return jnp.transpose(turned[array])

    causal = collect(0)
    mixed[...] = (query_ref[...].astype(F32) * causal).astype(BF16)
    send(mixed, mixed_ref)
    gquery[...] = (upstream_ref[...].astype(F32) * causal).astype(BF16)
    send(gquery, gquery_ref)
    back_conv = collect(1)
    gkey[...] = (back_conv * value_ref[...].astype(F32)).astype(BF16)
    send(gkey, gkey_ref)
    gvalue[...] = (back_conv * key_ref[...].astype(F32)).astype(BF16)
    send(gvalue, gvalue_ref)
    shares = decode(rows[chip_rows(GROUP_SLOT), :], scale_at(scales, GROUP_SLOT))
    parts = [shares[GROUPS * sub : GROUPS * (sub + 1)] for sub in range(SUBS)]
    gfilter[...] = (parts[0] + parts[1]) + (parts[2] + parts[3])
    send(gfilter, gfilter_ref)
    for copy in copies:
        copy.wait()


def swap_cores(values):
    count = lax.axis_size("inner")
    return lax.ppermute(values, "inner", [(i, i ^ 1) for i in range(count)])


def exchange(blocks):
    groups = [list(range(core, PIECES, 2)) for core in range(2)]
    return lax.all_to_all(
        blocks.reshape(CHIPS * SLOTS // 2, 2, ROWS),
        AXES,
        split_axis=0,
        concat_axis=0,
        tiled=True,
        axis_index_groups=groups,
    ).reshape(CHIPS * SLOTS, ROWS)


def per_device(gate_query, gate_key, value_input, filter_taps, grad_output):
    core = (lax.axis_index("inner") % 2).astype(jnp.int32).reshape(1)
    scalar = pl.BlockSpec(memory_space=pltpu.SMEM)
    whole = pl.BlockSpec(memory_space=pltpu.VMEM)
    small = pltpu.CompilerParams(vmem_limit_bytes=SMALL)
    packed = jax.ShapeDtypeStruct((CHIPS * SLOTS, ROWS), BF16)
    rows = pltpu.VMEM((CHIPS * SLOTS, ROWS), F32)
    turned = pltpu.VMEM((2, CHANNELS, ROWS), F32)
    far = pl.BlockSpec(memory_space=pltpu.HBM)
    wide = pltpu.VMEM((ROWS, CHANNELS), BF16)
    sources = (gate_query, gate_key, value_input, filter_taps, grad_output)
    blocks = pl.pallas_call(
        pack_kernel,
        out_shape=packed,
        in_specs=[far] * 5,
        out_specs=whole,
        scratch_shapes=[
            wide,
            wide,
            wide,
            pltpu.VMEM((GROUPS, ROWS), BF16),
            wide,
            turned,
            turned,
            rows,
            pltpu.SemaphoreType.DMA((5,)),
        ],
        compiler_params=small,
    )(*(pltpu.with_memory_space_constraint(source, pltpu.HBM) for source in sources))
    received = exchange(blocks)
    other = swap_cores(received)
    first, second, twist, last = (jnp.asarray(table) for table in tables())
    own = pl.pallas_call(
        own_kernel,
        out_shape=jax.ShapeDtypeStruct((PIECES, SLOTS * ROWS), F32),
        in_specs=[scalar, whole, whole],
        out_specs=whole,
        scratch_shapes=[rows],
        compiler_params=pltpu.CompilerParams(vmem_limit_bytes=LARGE),
    )(core, received, first)
    results = pl.pallas_call(
        convolve_kernel,
        out_shape=packed,
        in_specs=[scalar] + [whole] * 6,
        out_specs=whole,
        scratch_shapes=[rows],
        compiler_params=pltpu.CompilerParams(vmem_limit_bytes=LARGE),
    )(core, other, own, first, second, twist, last)
    out = jax.ShapeDtypeStruct((ROWS, CHANNELS), BF16)
    return pl.pallas_call(
        finish_kernel,
        out_shape=(out, out, out, out, jax.ShapeDtypeStruct((GROUPS, ROWS), F32)),
        in_specs=[whole] * 5,
        out_specs=(far,) * 5,
        scratch_shapes=[
            wide,
            wide,
            wide,
            wide,
            pltpu.VMEM((GROUPS, ROWS), F32),
            turned,
            rows,
            pltpu.SemaphoreType.DMA((5,)),
        ],
        compiler_params=small,
    )(exchange(results), gate_query, gate_key, value_input, grad_output)


def solution(mesh):
    rows = P(AXES, "chan")
    taps = P("chan", AXES)
    return jax.shard_map(
        per_device,
        mesh=mesh,
        in_specs=(rows, rows, rows, taps, rows),
        out_specs=(rows, rows, rows, rows, taps),
        check_vma=False,
    )
```

```python
import math

import jax
import jax.numpy as jnp
import numpy as np
from jax import lax
from jax.experimental import pallas as pl
from jax.experimental.pallas import tpu as pltpu
from jax.sharding import PartitionSpec as P

AXES = ("seq", "inner")
PIECES = 128
CHIPS = PIECES // 2
ROWS = 128
CHANNELS = 256
GROUPS = 16
SUBS = CHIPS // GROUPS
OWNED = 4
LENGTH = PIECES * ROWS
PADDED = 2 * LENGTH
OUTER = 2 * PIECES
GROUP_SLOT = 2 * OWNED
SCALE_SLOT = GROUP_SLOT + 1
SLOTS = SCALE_SLOT + 1
POWER = 64
RANGE = 125 / POWER
REACH = 2.0 ** (2 * RANGE) - 1.0
SHARE = 8
SMALL = 4 * 1024 * 1024
LARGE = 24 * 1024 * 1024
F32 = jnp.float32
BF16 = jnp.bfloat16


def split_table(table):
    high = table.astype(np.float32).astype(jnp.bfloat16)
    low = (table - high.astype(np.float64)).astype(jnp.bfloat16)
    return high, low


def tables():
    k1 = np.arange(OUTER)
    k1_half = np.arange(PIECES)
    t1 = np.stack((np.arange(0, PIECES, 2), np.arange(1, PIECES, 2)))
    t2 = np.arange(ROWS)
    outer = np.exp(-2j * np.pi * ((k1_half[None, :, None] * t1[:, None, :]) % OUTER) / OUTER)
    inner = np.exp(-2j * np.pi * ((t2[:, None] * t2[None, :]) % ROWS) / ROWS)
    twist = np.exp(-2j * np.pi * (k1[:, None] * t2[None, :]) / PADDED)
    first = np.concatenate((outer.real, outer.imag), axis=1)
    second = np.block([[inner.real, inner.imag], [-inner.imag, inner.real]])
    scale = 1.0 / (math.sqrt(LENGTH) * PADDED)
    last = np.swapaxes(np.concatenate((outer.real, outer.imag), axis=2), 1, 2) * scale
    first_high, first_low = split_table(first)
    second_high, second_low = split_table(second)
    last_high, last_low = split_table(last)
    return (
        np.concatenate((first_high, first_low, first_high), axis=2),
        np.concatenate((second_high, second_low), axis=0),
        np.stack((twist.real, twist.imag)).astype(np.float32),
        np.concatenate((last_high, last_low), axis=2),
    )


def split(values):
    high = values.astype(BF16)
    low = (values - high.astype(F32)).astype(BF16)
    return high, low


def dot(left, right):
    return jnp.dot(left, right, preferred_element_type=F32)


def scale_of(values, axis):
    peak = jnp.max(jnp.abs(values), axis=axis, keepdims=True)
    return (jnp.maximum(peak, 2.0**-118) * 1.0078125).astype(BF16).astype(F32)


def encode(values, scale):
    power = jnp.abs(values) * (REACH * 2.0**-RANGE / scale) + 2.0**-RANGE
    for _ in range(6):
        power = power * power
    return jnp.where(values < 0, -power, power)


def scale_at(scales, slot):
    return scales[:, SHARE * slot : SHARE * slot + 1]


def join_scales(scales):
    lane = lax.broadcasted_iota(jnp.int32, (scales[0].shape[0], ROWS), 1)
    joined = scales[0]
    for slot, scale in enumerate(scales[1:], 1):
        joined = jnp.where(lane < SHARE * slot, joined, scale)
    return joined


def decode(codes, scale):
    size = jnp.exp2(jnp.log2(jnp.abs(codes)) * (1.0 / POWER) + RANGE) - 1.0
    size = size * (scale * (1.0 / REACH))
    return jnp.where(codes < 0, -size, size)


def chip_rows(slot, first=0, count=CHIPS):
    return pl.ds(first * SLOTS + slot, count, stride=SLOTS)


def slot_of(array, owned):
    return 4 * (owned // 2) + 2 * array + owned % 2


def pack_kernel(
    query_ref, key_ref, value_ref, taps_ref, upstream_ref, out_ref, query, key, value, taps, upstream, turned, scaled, rows, sems
):
    moves = (
        (key_ref, key),
        (value_ref, value),
        (upstream_ref, upstream),
        (query_ref, query),
        (taps_ref, taps),
    )
    copies = [pltpu.make_async_copy(a, b, sems.at[i]) for i, (a, b) in enumerate(moves)]
    for copy in copies:
        copy.start()

    def place(array, left, right):
        product = left[...].astype(F32) * right[...].astype(F32)
        scale = scale_of(product, axis=0)
        codes = encode(product, scale).astype(BF16)
        turned[array] = jnp.transpose(codes).astype(F32)
        wide_scale = jnp.broadcast_to(scale.astype(BF16), (ROWS, CHANNELS))
        scaled[array] = jnp.transpose(wide_scale).astype(F32)
        for owned in range(OWNED):
            for sub in range(SUBS):
                rows[chip_rows(slot_of(array, owned), GROUPS * sub, GROUPS), :] = turned[
                    array, pl.ds(SUBS * owned + sub, GROUPS, stride=GROUPS), :
                ]

    copies[0].wait()
    copies[1].wait()
    place(0, key, value)
    copies[2].wait()
    copies[3].wait()
    place(1, upstream, query)
    copies[4].wait()
    for sub in range(SUBS):
        rows[chip_rows(GROUP_SLOT, GROUPS * sub, GROUPS), :] = taps[...].astype(F32)
        scales = [None] * GROUP_SLOT
        for array in range(2):
            for owned in range(OWNED):
                scales[slot_of(array, owned)] = scaled[
                    array, pl.ds(SUBS * owned + sub, GROUPS, stride=GROUPS), :
                ]
        rows[chip_rows(SCALE_SLOT, GROUPS * sub, GROUPS), :] = join_scales(scales)
    out_ref[...] = rows[...].astype(BF16)


def outer_forward(in_ref, rows, table):
    rows[...] = in_ref[...].astype(F32)
    scales = rows[chip_rows(SCALE_SLOT), :]

    def transform(values):
        high, low = split(values)
        mixed = dot(table, jnp.concatenate((high, high, low), axis=0))
        return mixed[:PIECES], mixed[PIECES:]

    taps = transform(rows[chip_rows(GROUP_SLOT), :])
    results = []
    for first in range(0, GROUP_SLOT, 2):
        pair = [decode(rows[chip_rows(slot), :], scale_at(scales, slot)) for slot in (first, first + 1)]
        cosines, sines = transform(jnp.concatenate(pair, axis=1))
        results.append(
            (cosines[:, :ROWS] - sines[:, ROWS:], sines[:, :ROWS] + cosines[:, ROWS:])
        )
    return results + [taps]


def own_kernel(core_ref, in_ref, first_ref, out_ref, rows):
    for index, (real, imag) in enumerate(outer_forward(in_ref, rows, first_ref[core_ref[0]])):
        out_ref[:, 2 * index * ROWS : (2 * index + 1) * ROWS] = real
        out_ref[:, (2 * index + 1) * ROWS : (2 * index + 2) * ROWS] = imag


def convolve_kernel(core_ref, other_ref, own_ref, first_ref, second_ref, twist_ref, last_ref, out_ref, rows):
    core = core_ref[0]
    sign = (1 - 2 * core).astype(F32)
    second = jnp.concatenate(
        (second_ref[: 2 * ROWS], second_ref[: 2 * ROWS], second_ref[2 * ROWS :]), axis=0
    )
    table = last_ref[core]
    last = jnp.concatenate((table[:, :PIECES], table[:, :PIECES], table[:, PIECES:]), axis=1)
    twist_real, twist_imag = (
        jnp.concatenate((twist_ref[i, :PIECES], sign * twist_ref[i, PIECES:]), axis=0) for i in range(2)
    )

    def rotate(real, imag, way):
        return (
            real * twist_real - way * (imag * twist_imag),
            imag * twist_real + way * (real * twist_imag),
        )

    def inner(real, imag):
        high, low = split(jnp.concatenate((real, imag), axis=1))
        result = dot(jnp.concatenate((high, low, high), axis=1), second)
        return result[:, :ROWS], result[:, ROWS:]

    def both(index, part, other):
        column = (2 * index + part) * ROWS
        own = own_ref[:, column : column + ROWS]
        return jnp.concatenate((own + other, own - other), axis=0)

    def forward(index, real, imag):
        return inner(*rotate(both(index, 0, real), both(index, 1, imag), 1.0))

    def back(real, imag):
        turned_imag, turned_real = inner(imag, real)
        turned = jnp.concatenate(rotate(turned_real, turned_imag, -1.0), axis=1)
        return turned[:PIECES] + turned[PIECES:]

    others = outer_forward(other_ref, rows, first_ref[1 - core])
    taps_real, taps_imag = forward(4, *others[4])

    def with_taps(real, imag):
        return back(
            real * taps_real - imag * taps_imag,
            real * taps_imag + imag * taps_real,
        )

    def against_taps(real, imag):
        return back(
            real * taps_real + imag * taps_imag,
            imag * taps_real - real * taps_imag,
        )

    values, grads = [None] * 2, [None] * 2
    values[0] = forward(0, *others[0])
    grads[0] = forward(1, *others[1])
    values[1] = forward(2, *others[2])
    spectra = [with_taps(*values[0])]
    grads[1] = forward(3, *others[3])
    spectra.append(against_taps(*grads[0]))
    spectra.append(with_taps(*values[1]))
    spectra.append(against_taps(*grads[1]))
    cross_real = cross_imag = 0.0
    for (value_real, value_imag), (grad_real, grad_imag) in zip(values, grads):
        cross_real = cross_real + (grad_real * value_real + grad_imag * value_imag)
        cross_imag = cross_imag + (grad_imag * value_real - grad_real * value_imag)
    spectra.append(back(cross_real, cross_imag))
    high, low = split(jnp.concatenate(spectra, axis=1))
    final = dot(last, jnp.concatenate((high, low, high), axis=0))

    def block(half, index):
        return final[half * CHIPS : (half + 1) * CHIPS, index * ROWS : (index + 1) * ROWS]

    results = []
    for slot in range(0, GROUP_SLOT, 2):
        results.append(block(0, slot) + block(1, slot + 1))
        results.append(block(0, slot + 1) - block(1, slot))
    results.append(block(0, GROUP_SLOT) + block(1, GROUP_SLOT + 1))
    scales = [scale_of(result, axis=1) for result in results]
    for slot, result in enumerate(results):
        rows[chip_rows(slot), :] = encode(result, scales[slot])
    rows[chip_rows(SCALE_SLOT), :] = join_scales(
        [jnp.broadcast_to(scale, (CHIPS, ROWS)) for scale in scales]
    )
    out_ref[...] = rows[...].astype(BF16)


def finish_kernel(
    in_ref,
    query_ref,
    key_ref,
    value_ref,
    upstream_ref,
    mixed_ref,
    gquery_ref,
    gkey_ref,
    gvalue_ref,
    gfilter_ref,
    mixed,
    gquery,
    gkey,
    gvalue,
    gfilter,
    turned,
    rows,
    sems,
):
    copies = []

    def send(source, target):
        copy = pltpu.make_async_copy(source, target, sems.at[len(copies)])
        copy.start()
        copies.append(copy)

    rows[...] = in_ref[...].astype(F32)
    scales = rows[chip_rows(SCALE_SLOT), :]

    def collect(array):
        for owned in range(OWNED):
            slot = slot_of(array, owned)
            values = decode(rows[chip_rows(slot), :], scale_at(scales, slot))
            for sub in range(SUBS):
                turned[array, pl.ds(SUBS * owned + sub, GROUPS, stride=GROUPS), :] = values[
                    GROUPS * sub : GROUPS * (sub + 1)
                ]
        return jnp.transpose(turned[array])

    causal = collect(0)
    mixed[...] = (query_ref[...].astype(F32) * causal).astype(BF16)
    send(mixed, mixed_ref)
    gquery[...] = (upstream_ref[...].astype(F32) * causal).astype(BF16)
    send(gquery, gquery_ref)
    back_conv = collect(1)
    gkey[...] = (back_conv * value_ref[...].astype(F32)).astype(BF16)
    send(gkey, gkey_ref)
    gvalue[...] = (back_conv * key_ref[...].astype(F32)).astype(BF16)
    send(gvalue, gvalue_ref)
    shares = decode(rows[chip_rows(GROUP_SLOT), :], scale_at(scales, GROUP_SLOT))
    parts = [shares[GROUPS * sub : GROUPS * (sub + 1)] for sub in range(SUBS)]
    gfilter[...] = (parts[0] + parts[1]) + (parts[2] + parts[3])
    send(gfilter, gfilter_ref)
    for copy in copies:
        copy.wait()


def swap_cores(values):
    count = lax.axis_size("inner")
    return lax.ppermute(values, "inner", [(i, i ^ 1) for i in range(count)])


def exchange(blocks):
    groups = [list(range(core, PIECES, 2)) for core in range(2)]
    return lax.all_to_all(
        blocks.reshape(CHIPS * SLOTS // 2, 2, ROWS),
        AXES,
        split_axis=0,
        concat_axis=0,
        tiled=True,
        axis_index_groups=groups,
    ).reshape(CHIPS * SLOTS, ROWS)


def per_device(gate_query, gate_key, value_input, filter_taps, grad_output):
    core = (lax.axis_index("inner") % 2).astype(jnp.int32).reshape(1)
    scalar = pl.BlockSpec(memory_space=pltpu.SMEM)
    whole = pl.BlockSpec(memory_space=pltpu.VMEM)
    small = pltpu.CompilerParams(vmem_limit_bytes=SMALL)
    packed = jax.ShapeDtypeStruct((CHIPS * SLOTS, ROWS), BF16)
    rows = pltpu.VMEM((CHIPS * SLOTS, ROWS), F32)
    turned = pltpu.VMEM((2, CHANNELS, ROWS), F32)
    far = pl.BlockSpec(memory_space=pltpu.HBM)
    wide = pltpu.VMEM((ROWS, CHANNELS), BF16)
    sources = (gate_query, gate_key, value_input, filter_taps, grad_output)
    blocks = pl.pallas_call(
        pack_kernel,
        out_shape=packed,
        in_specs=[far] * 5,
        out_specs=whole,
        scratch_shapes=[
            wide,
            wide,
            wide,
            pltpu.VMEM((GROUPS, ROWS), BF16),
            wide,
            turned,
            turned,
            rows,
            pltpu.SemaphoreType.DMA((5,)),
        ],
        compiler_params=small,
    )(*(pltpu.with_memory_space_constraint(source, pltpu.HBM) for source in sources))
    received = exchange(blocks)
    other = swap_cores(received)
    first, second, twist, last = (jnp.asarray(table) for table in tables())
    own = pl.pallas_call(
        own_kernel,
        out_shape=jax.ShapeDtypeStruct((PIECES, SLOTS * ROWS), F32),
        in_specs=[scalar, whole, whole],
        out_specs=whole,
        scratch_shapes=[rows],
        compiler_params=pltpu.CompilerParams(vmem_limit_bytes=LARGE),
    )(core, received, first)
    results = pl.pallas_call(
        convolve_kernel,
        out_shape=packed,
        in_specs=[scalar] + [whole] * 6,
        out_specs=whole,
        scratch_shapes=[rows],
        compiler_params=pltpu.CompilerParams(vmem_limit_bytes=LARGE),
    )(core, other, own, first, second, twist, last)
    out = jax.ShapeDtypeStruct((ROWS, CHANNELS), BF16)
    return pl.pallas_call(
        finish_kernel,
        out_shape=(out, out, out, out, jax.ShapeDtypeStruct((GROUPS, ROWS), F32)),
        in_specs=[whole] * 5,
        out_specs=(far,) * 5,
        scratch_shapes=[
            wide,
            wide,
            wide,
            wide,
            pltpu.VMEM((GROUPS, ROWS), F32),
            turned,
            rows,
            pltpu.SemaphoreType.DMA((5,)),
        ],
        compiler_params=small,
    )(exchange(results), gate_query, gate_key, value_input, grad_output)


def solution(mesh):
    rows = P(AXES, "chan")
    taps = P("chan", AXES)
    return jax.shard_map(
        per_device,
        mesh=mesh,
        in_specs=(rows, rows, rows, taps, rows),
        out_specs=(rows, rows, rows, rows, taps),
        check_vma=False,
    )
```

```python
import math

import jax
import jax.numpy as jnp
import numpy as np
from jax import lax
from jax.experimental import pallas as pl
from jax.experimental.pallas import tpu as pltpu
from jax.sharding import PartitionSpec as P

AXES = ("seq", "inner")
PIECES = 128
CHIPS = PIECES // 2
ROWS = 128
CHANNELS = 256
GROUPS = 16
SUBS = CHIPS // GROUPS
OWNED = 4
LENGTH = PIECES * ROWS
PADDED = 2 * LENGTH
OUTER = 2 * PIECES
GROUP_SLOT = 2 * OWNED
SCALE_SLOT = GROUP_SLOT + 1
SLOTS = SCALE_SLOT + 1
POWER = 64
RANGE = 125 / POWER
REACH = 2.0 ** (2 * RANGE) - 1.0
SHARE = 8
SMALL = 4 * 1024 * 1024
LARGE = 24 * 1024 * 1024
F32 = jnp.float32
BF16 = jnp.bfloat16


def split_table(table):
    high = table.astype(np.float32).astype(jnp.bfloat16)
    low = (table - high.astype(np.float64)).astype(jnp.bfloat16)
    return high, low


def tables():
    k1 = np.arange(OUTER)
    k1_half = np.arange(PIECES)
    t1 = np.stack((np.arange(0, PIECES, 2), np.arange(1, PIECES, 2)))
    t2 = np.arange(ROWS)
    outer = np.exp(-2j * np.pi * ((k1_half[None, :, None] * t1[:, None, :]) % OUTER) / OUTER)
    inner = np.exp(-2j * np.pi * ((t2[:, None] * t2[None, :]) % ROWS) / ROWS)
    twist = np.exp(-2j * np.pi * (k1[:, None] * t2[None, :]) / PADDED)
    first = np.concatenate((outer.real, outer.imag), axis=1)
    second = np.block([[inner.real, inner.imag], [-inner.imag, inner.real]])
    scale = 1.0 / (math.sqrt(LENGTH) * PADDED)
    last = np.swapaxes(np.concatenate((outer.real, outer.imag), axis=2), 1, 2) * scale
    first_high, first_low = split_table(first)
    second_high, second_low = split_table(second)
    last_high, last_low = split_table(last)
    return (
        np.concatenate((first_high, first_low, first_high), axis=2),
        np.concatenate((second_high, second_low), axis=0),
        np.stack((twist.real, twist.imag)).astype(np.float32),
        np.concatenate((last_high, last_low), axis=2),
    )


def split(values):
    high = values.astype(BF16)
    low = (values - high.astype(F32)).astype(BF16)
    return high, low


def dot(left, right):
    return jnp.dot(left, right, preferred_element_type=F32)


def scale_of(values, axis):
    peak = jnp.max(jnp.abs(values), axis=axis, keepdims=True)
    return (jnp.maximum(peak, 2.0**-118) * 1.0078125).astype(BF16).astype(F32)


def encode(values, scale):
    power = jnp.abs(values) * (REACH * 2.0**-RANGE / scale) + 2.0**-RANGE
    for _ in range(6):
        power = power * power
    return jnp.where(values < 0, -power, power)


def scale_at(scales, slot):
    return scales[:, SHARE * slot : SHARE * slot + 1]


def join_scales(scales):
    lane = lax.broadcasted_iota(jnp.int32, (scales[0].shape[0], ROWS), 1)
    joined = scales[0]
    for slot, scale in enumerate(scales[1:], 1):
        joined = jnp.where(lane < SHARE * slot, joined, scale)
    return joined


def decode(codes, scale):
    size = jnp.exp2(jnp.log2(jnp.abs(codes)) * (1.0 / POWER) + RANGE) - 1.0
    size = size * (scale * (1.0 / REACH))
    return jnp.where(codes < 0, -size, size)


def chip_rows(slot, first=0, count=CHIPS):
    return pl.ds(first * SLOTS + slot, count, stride=SLOTS)


def slot_of(array, owned):
    return 4 * (owned // 2) + 2 * array + owned % 2


def pack_kernel(
    query_ref, key_ref, value_ref, taps_ref, upstream_ref, out_ref, query, key, value, taps, upstream, turned, scaled, rows, sems
):
    moves = (
        (key_ref, key),
        (value_ref, value),
        (upstream_ref, upstream),
        (query_ref, query),
        (taps_ref, taps),
    )
    copies = [pltpu.make_async_copy(a, b, sems.at[i]) for i, (a, b) in enumerate(moves)]
    for copy in copies:
        copy.start()

    def place(array, left, right):
        product = left[...].astype(F32) * right[...].astype(F32)
        scale = scale_of(product, axis=0)
        codes = encode(product, scale).astype(BF16)
        turned[array] = jnp.transpose(codes).astype(F32)
        wide_scale = jnp.broadcast_to(scale.astype(BF16), (ROWS, CHANNELS))
        scaled[array] = jnp.transpose(wide_scale).astype(F32)
        for owned in range(OWNED):
            for sub in range(SUBS):
                rows[chip_rows(slot_of(array, owned), GROUPS * sub, GROUPS), :] = turned[
                    array, pl.ds(SUBS * owned + sub, GROUPS, stride=GROUPS), :
                ]

    for copy in copies:
        copy.wait()
    place(0, key, value)
    place(1, upstream, query)
    for sub in range(SUBS):
        rows[chip_rows(GROUP_SLOT, GROUPS * sub, GROUPS), :] = taps[...].astype(F32)
        scales = [None] * GROUP_SLOT
        for array in range(2):
            for owned in range(OWNED):
                scales[slot_of(array, owned)] = scaled[
                    array, pl.ds(SUBS * owned + sub, GROUPS, stride=GROUPS), :
                ]
        rows[chip_rows(SCALE_SLOT, GROUPS * sub, GROUPS), :] = join_scales(scales)
    out_ref[...] = rows[...].astype(BF16)


def outer_forward(in_ref, rows, table):
    rows[...] = in_ref[...].astype(F32)
    scales = rows[chip_rows(SCALE_SLOT), :]

    def transform(values):
        high, low = split(values)
        mixed = dot(table, jnp.concatenate((high, high, low), axis=0))
        return mixed[:PIECES], mixed[PIECES:]

    taps = transform(rows[chip_rows(GROUP_SLOT), :])
    results = []
    for first in range(0, GROUP_SLOT, 2):
        pair = [decode(rows[chip_rows(slot), :], scale_at(scales, slot)) for slot in (first, first + 1)]
        cosines, sines = transform(jnp.concatenate(pair, axis=1))
        results.append(
            (cosines[:, :ROWS] - sines[:, ROWS:], sines[:, :ROWS] + cosines[:, ROWS:])
        )
    return results + [taps]


def own_kernel(core_ref, in_ref, first_ref, out_ref, rows):
    for index, (real, imag) in enumerate(outer_forward(in_ref, rows, first_ref[core_ref[0]])):
        out_ref[:, 2 * index * ROWS : (2 * index + 1) * ROWS] = real
        out_ref[:, (2 * index + 1) * ROWS : (2 * index + 2) * ROWS] = imag


def convolve_kernel(core_ref, other_ref, own_ref, first_ref, second_ref, twist_ref, last_ref, out_ref, rows):
    core = core_ref[0]
    sign = (1 - 2 * core).astype(F32)
    second = jnp.concatenate(
        (second_ref[: 2 * ROWS], second_ref[: 2 * ROWS], second_ref[2 * ROWS :]), axis=0
    )
    table = last_ref[core]
    last = jnp.concatenate((table[:, :PIECES], table[:, :PIECES], table[:, PIECES:]), axis=1)
    twist_real, twist_imag = (
        jnp.concatenate((twist_ref[i, :PIECES], sign * twist_ref[i, PIECES:]), axis=0) for i in range(2)
    )

    def rotate(real, imag, way):
        return (
            real * twist_real - way * (imag * twist_imag),
            imag * twist_real + way * (real * twist_imag),
        )

    def inner(real, imag):
        high, low = split(jnp.concatenate((real, imag), axis=1))
        result = dot(jnp.concatenate((high, low, high), axis=1), second)
        return result[:, :ROWS], result[:, ROWS:]

    def both(index, part, other):
        column = (2 * index + part) * ROWS
        own = own_ref[:, column : column + ROWS]
        return jnp.concatenate((own + other, own - other), axis=0)

    def forward(index, real, imag):
        return inner(*rotate(both(index, 0, real), both(index, 1, imag), 1.0))

    def back(real, imag):
        turned_imag, turned_real = inner(imag, real)
        turned = jnp.concatenate(rotate(turned_real, turned_imag, -1.0), axis=1)
        return turned[:PIECES] + turned[PIECES:]

    others = outer_forward(other_ref, rows, first_ref[1 - core])
    taps_real, taps_imag = forward(4, *others[4])

    def with_taps(real, imag):
        return back(
            real * taps_real - imag * taps_imag,
            real * taps_imag + imag * taps_real,
        )

    def against_taps(real, imag):
        return back(
            real * taps_real + imag * taps_imag,
            imag * taps_real - real * taps_imag,
        )

    values, grads = [None] * 2, [None] * 2
    values[0] = forward(0, *others[0])
    grads[0] = forward(1, *others[1])
    values[1] = forward(2, *others[2])
    spectra = [with_taps(*values[0])]
    grads[1] = forward(3, *others[3])
    spectra.append(against_taps(*grads[0]))
    spectra.append(with_taps(*values[1]))
    spectra.append(against_taps(*grads[1]))
    cross_real = cross_imag = 0.0
    for (value_real, value_imag), (grad_real, grad_imag) in zip(values, grads):
        cross_real = cross_real + (grad_real * value_real + grad_imag * value_imag)
        cross_imag = cross_imag + (grad_imag * value_real - grad_real * value_imag)
    spectra.append(back(cross_real, cross_imag))
    high, low = split(jnp.concatenate(spectra, axis=1))
    final = dot(last, jnp.concatenate((high, low, high), axis=0))

    def block(half, index):
        return final[half * CHIPS : (half + 1) * CHIPS, index * ROWS : (index + 1) * ROWS]

    results = []
    for slot in range(0, GROUP_SLOT, 2):
        results.append(block(0, slot) + block(1, slot + 1))
        results.append(block(0, slot + 1) - block(1, slot))
    results.append(block(0, GROUP_SLOT) + block(1, GROUP_SLOT + 1))
    scales = [scale_of(result, axis=1) for result in results]
    for slot, result in enumerate(results):
        rows[chip_rows(slot), :] = encode(result, scales[slot])
    rows[chip_rows(SCALE_SLOT), :] = join_scales(
        [jnp.broadcast_to(scale, (CHIPS, ROWS)) for scale in scales]
    )
    out_ref[...] = rows[...].astype(BF16)


def finish_kernel(
    in_ref,
    query_ref,
    key_ref,
    value_ref,
    upstream_ref,
    mixed_ref,
    gquery_ref,
    gkey_ref,
    gvalue_ref,
    gfilter_ref,
    mixed,
    gquery,
    gkey,
    gvalue,
    gfilter,
    turned,
    rows,
    sems,
):
    rows[...] = in_ref[...].astype(F32)
    scales = rows[chip_rows(SCALE_SLOT), :]

    def collect(array):
        for owned in range(OWNED):
            slot = slot_of(array, owned)
            values = decode(rows[chip_rows(slot), :], scale_at(scales, slot))
            for sub in range(SUBS):
                turned[array, pl.ds(SUBS * owned + sub, GROUPS, stride=GROUPS), :] = values[
                    GROUPS * sub : GROUPS * (sub + 1)
                ]
        return jnp.transpose(turned[array])

    shares = decode(rows[chip_rows(GROUP_SLOT), :], scale_at(scales, GROUP_SLOT))
    parts = [shares[GROUPS * sub : GROUPS * (sub + 1)] for sub in range(SUBS)]
    gfilter[...] = (parts[0] + parts[1]) + (parts[2] + parts[3])
    causal = collect(0)
    back_conv = collect(1)
    mixed[...] = (query_ref[...].astype(F32) * causal).astype(BF16)
    gquery[...] = (upstream_ref[...].astype(F32) * causal).astype(BF16)
    gkey[...] = (back_conv * value_ref[...].astype(F32)).astype(BF16)
    gvalue[...] = (back_conv * key_ref[...].astype(F32)).astype(BF16)
    moves = (
        (mixed, mixed_ref),
        (gquery, gquery_ref),
        (gkey, gkey_ref),
        (gvalue, gvalue_ref),
        (gfilter, gfilter_ref),
    )
    copies = [pltpu.make_async_copy(a, b, sems.at[i]) for i, (a, b) in enumerate(moves)]
    for copy in copies:
        copy.start()
    for copy in copies:
        copy.wait()


def swap_cores(values):
    count = lax.axis_size("inner")
    return lax.ppermute(values, "inner", [(i, i ^ 1) for i in range(count)])


def exchange(blocks):
    groups = [list(range(core, PIECES, 2)) for core in range(2)]
    return lax.all_to_all(
        blocks.reshape(CHIPS * SLOTS // 2, 2, ROWS),
        AXES,
        split_axis=0,
        concat_axis=0,
        tiled=True,
        axis_index_groups=groups,
    ).reshape(CHIPS * SLOTS, ROWS)


def per_device(gate_query, gate_key, value_input, filter_taps, grad_output):
    core = (lax.axis_index("inner") % 2).astype(jnp.int32).reshape(1)
    scalar = pl.BlockSpec(memory_space=pltpu.SMEM)
    whole = pl.BlockSpec(memory_space=pltpu.VMEM)
    small = pltpu.CompilerParams(vmem_limit_bytes=SMALL)
    packed = jax.ShapeDtypeStruct((CHIPS * SLOTS, ROWS), BF16)
    rows = pltpu.VMEM((CHIPS * SLOTS, ROWS), F32)
    turned = pltpu.VMEM((2, CHANNELS, ROWS), F32)
    far = pl.BlockSpec(memory_space=pltpu.HBM)
    wide = pltpu.VMEM((ROWS, CHANNELS), BF16)
    sources = (gate_query, gate_key, value_input, filter_taps, grad_output)
    blocks = pl.pallas_call(
        pack_kernel,
        out_shape=packed,
        in_specs=[far] * 5,
        out_specs=whole,
        scratch_shapes=[
            wide,
            wide,
            wide,
            pltpu.VMEM((GROUPS, ROWS), BF16),
            wide,
            turned,
            turned,
            rows,
            pltpu.SemaphoreType.DMA((5,)),
        ],
        compiler_params=small,
    )(*(pltpu.with_memory_space_constraint(source, pltpu.HBM) for source in sources))
    received = exchange(blocks)
    other = swap_cores(received)
    first, second, twist, last = (jnp.asarray(table) for table in tables())
    own = pl.pallas_call(
        own_kernel,
        out_shape=jax.ShapeDtypeStruct((PIECES, SLOTS * ROWS), F32),
        in_specs=[scalar, whole, whole],
        out_specs=whole,
        scratch_shapes=[rows],
        compiler_params=pltpu.CompilerParams(vmem_limit_bytes=LARGE),
    )(core, received, first)
    results = pl.pallas_call(
        convolve_kernel,
        out_shape=packed,
        in_specs=[scalar] + [whole] * 6,
        out_specs=whole,
        scratch_shapes=[rows],
        compiler_params=pltpu.CompilerParams(vmem_limit_bytes=LARGE),
    )(core, other, own, first, second, twist, last)
    out = jax.ShapeDtypeStruct((ROWS, CHANNELS), BF16)
    return pl.pallas_call(
        finish_kernel,
        out_shape=(out, out, out, out, jax.ShapeDtypeStruct((GROUPS, ROWS), F32)),
        in_specs=[whole] * 5,
        out_specs=(far,) * 5,
        scratch_shapes=[
            wide,
            wide,
            wide,
            wide,
            pltpu.VMEM((GROUPS, ROWS), F32),
            turned,
            rows,
            pltpu.SemaphoreType.DMA((5,)),
        ],
        compiler_params=small,
    )(exchange(results), gate_query, gate_key, value_input, grad_output)


def solution(mesh):
    rows = P(AXES, "chan")
    taps = P("chan", AXES)
    return jax.shard_map(
        per_device,
        mesh=mesh,
        in_specs=(rows, rows, rows, taps, rows),
        out_specs=(rows, rows, rows, rows, taps),
        check_vma=False,
    )
```

```python
import math

import jax
import jax.numpy as jnp
import numpy as np
from jax import lax
from jax.experimental import pallas as pl
from jax.experimental.pallas import tpu as pltpu
from jax.sharding import PartitionSpec as P

AXES = ("seq", "inner")
PIECES = 128
CHIPS = PIECES // 2
ROWS = 128
CHANNELS = 256
GROUPS = 16
SUBS = CHIPS // GROUPS
OWNED = 4
LENGTH = PIECES * ROWS
PADDED = 2 * LENGTH
OUTER = 2 * PIECES
GROUP_SLOT = 2 * OWNED
SCALE_SLOT = GROUP_SLOT + 1
SLOTS = SCALE_SLOT + 1
POWER = 64
RANGE = 125 / POWER
REACH = 2.0 ** (2 * RANGE) - 1.0
SHARE = 8
SMALL = 4 * 1024 * 1024
LARGE = 24 * 1024 * 1024
F32 = jnp.float32
BF16 = jnp.bfloat16


def split_table(table):
    high = table.astype(np.float32).astype(jnp.bfloat16)
    low = (table - high.astype(np.float64)).astype(jnp.bfloat16)
    return high, low


def tables():
    k1 = np.arange(OUTER)
    k1_half = np.arange(PIECES)
    t1 = np.stack((np.arange(0, PIECES, 2), np.arange(1, PIECES, 2)))
    t2 = np.arange(ROWS)
    outer = np.exp(-2j * np.pi * ((k1_half[None, :, None] * t1[:, None, :]) % OUTER) / OUTER)
    inner = np.exp(-2j * np.pi * ((t2[:, None] * t2[None, :]) % ROWS) / ROWS)
    twist = np.exp(-2j * np.pi * (k1[:, None] * t2[None, :]) / PADDED)
    first = np.concatenate((outer.real, outer.imag), axis=1)
    second = np.block([[inner.real, inner.imag], [-inner.imag, inner.real]])
    scale = 1.0 / (math.sqrt(LENGTH) * PADDED)
    last = np.swapaxes(np.concatenate((outer.real, outer.imag), axis=2), 1, 2) * scale
    first_high, first_low = split_table(first)
    second_high, second_low = split_table(second)
    last_high, last_low = split_table(last)
    return (
        np.concatenate((first_high, first_low, first_high), axis=2),
        np.concatenate((second_high, second_low), axis=0),
        np.stack((twist.real, twist.imag)).astype(np.float32),
        np.concatenate((last_high, last_low), axis=2),
    )


def split(values):
    high = values.astype(BF16)
    low = (values - high.astype(F32)).astype(BF16)
    return high, low


def dot(left, right):
    return jnp.dot(left, right, preferred_element_type=F32)


def scale_of(values, axis):
    peak = jnp.max(jnp.abs(values), axis=axis, keepdims=True)
    return (jnp.maximum(peak, 2.0**-118) * 1.0078125).astype(BF16).astype(F32)


def encode(values, scale):
    power = jnp.abs(values) * (REACH * 2.0**-RANGE / scale) + 2.0**-RANGE
    for _ in range(6):
        power = power * power
    return jnp.where(values < 0, -power, power)


def scale_at(scales, slot):
    return scales[:, SHARE * slot : SHARE * slot + 1]


def join_scales(scales):
    lane = lax.broadcasted_iota(jnp.int32, (scales[0].shape[0], ROWS), 1)
    joined = scales[0]
    for slot, scale in enumerate(scales[1:], 1):
        joined = jnp.where(lane < SHARE * slot, joined, scale)
    return joined


def decode(codes, scale):
    size = jnp.exp2(jnp.log2(jnp.abs(codes)) * (1.0 / POWER) + RANGE) - 1.0
    size = size * (scale * (1.0 / REACH))
    return jnp.where(codes < 0, -size, size)


def chip_rows(slot, first=0, count=CHIPS):
    return pl.ds(first * SLOTS + slot, count, stride=SLOTS)


def slot_of(array, owned):
    return 4 * (owned // 2) + 2 * array + owned % 2


def pack_kernel(
    query_ref, key_ref, value_ref, taps_ref, upstream_ref, out_ref, query, key, value, taps, upstream, turned, scaled, rows, sems
):
    moves = (
        (key_ref, key),
        (value_ref, value),
        (upstream_ref, upstream),
        (query_ref, query),
        (taps_ref, taps),
    )
    copies = [pltpu.make_async_copy(a, b, sems.at[i]) for i, (a, b) in enumerate(moves)]
    for copy in copies:
        copy.start()

    def place(array, left, right):
        product = left[...].astype(F32) * right[...].astype(F32)
        scale = scale_of(product, axis=0)
        codes = encode(product, scale).astype(BF16)
        turned[array] = jnp.transpose(codes).astype(F32)
        wide_scale = jnp.broadcast_to(scale.astype(BF16), (ROWS, CHANNELS))
        scaled[array] = jnp.transpose(wide_scale).astype(F32)
        for owned in range(OWNED):
            for sub in range(SUBS):
                rows[chip_rows(slot_of(array, owned), GROUPS * sub, GROUPS), :] = turned[
                    array, pl.ds(SUBS * owned + sub, GROUPS, stride=GROUPS), :
                ]

    for copy in copies:
        copy.wait()
    place(0, key, value)
    place(1, upstream, query)
    for sub in range(SUBS):
        rows[chip_rows(GROUP_SLOT, GROUPS * sub, GROUPS), :] = taps[...].astype(F32)
        scales = [None] * GROUP_SLOT
        for array in range(2):
            for owned in range(OWNED):
                scales[slot_of(array, owned)] = scaled[
                    array, pl.ds(SUBS * owned + sub, GROUPS, stride=GROUPS), :
                ]
        rows[chip_rows(SCALE_SLOT, GROUPS * sub, GROUPS), :] = join_scales(scales)
    out_ref[...] = rows[...].astype(BF16)


def outer_forward(in_ref, rows, table):
    rows[...] = in_ref[...].astype(F32)
    scales = rows[chip_rows(SCALE_SLOT), :]

    def transform(values):
        high, low = split(values)
        mixed = dot(table, jnp.concatenate((high, high, low), axis=0))
        return mixed[:PIECES], mixed[PIECES:]

    taps = transform(rows[chip_rows(GROUP_SLOT), :])
    results = []
    for first in range(0, GROUP_SLOT, 2):
        pair = [decode(rows[chip_rows(slot), :], scale_at(scales, slot)) for slot in (first, first + 1)]
        cosines, sines = transform(jnp.concatenate(pair, axis=1))
        results.append(
            (cosines[:, :ROWS] - sines[:, ROWS:], sines[:, :ROWS] + cosines[:, ROWS:])
        )
    return results + [taps]


def own_kernel(core_ref, in_ref, first_ref, out_ref, rows):
    for index, (real, imag) in enumerate(outer_forward(in_ref, rows, first_ref[core_ref[0]])):
        out_ref[:, 2 * index * ROWS : (2 * index + 1) * ROWS] = real
        out_ref[:, (2 * index + 1) * ROWS : (2 * index + 2) * ROWS] = imag


def convolve_kernel(core_ref, other_ref, own_ref, first_ref, second_ref, twist_ref, last_ref, out_ref, rows):
    core = core_ref[0]
    sign = (1 - 2 * core).astype(F32)
    second = jnp.concatenate(
        (second_ref[: 2 * ROWS], second_ref[: 2 * ROWS], second_ref[2 * ROWS :]), axis=0
    )
    table = last_ref[core]
    last = jnp.concatenate((table[:, :PIECES], table[:, :PIECES], table[:, PIECES:]), axis=1)
    twist_real, twist_imag = (
        jnp.concatenate((twist_ref[i, :PIECES], sign * twist_ref[i, PIECES:]), axis=0) for i in range(2)
    )

    def rotate(real, imag, way):
        return (
            real * twist_real - way * (imag * twist_imag),
            imag * twist_real + way * (real * twist_imag),
        )

    def inner(*sequences):
        whole = jnp.concatenate([jnp.concatenate(parts, axis=1) for parts in sequences], axis=0)
        high, low = split(whole)
        result = dot(jnp.concatenate((high, low, high), axis=1), second)
        return [
            (result[start : start + OUTER, :ROWS], result[start : start + OUTER, ROWS:])
            for start in range(0, len(sequences) * OUTER, OUTER)
        ]

    def both(index, part):
        column = (2 * index + part) * ROWS
        own, other = own_ref[:, column : column + ROWS], others[index][part]
        return jnp.concatenate((own + other, own - other), axis=0)

    def forward(*indices):
        return inner(*(rotate(both(index, 0), both(index, 1), 1.0) for index in indices))

    def back(*spectra):
        halves = []
        for turned_imag, turned_real in inner(*((imag, real) for real, imag in spectra)):
            turned = jnp.concatenate(rotate(turned_real, turned_imag, -1.0), axis=1)
            halves.append(turned[:PIECES] + turned[PIECES:])
        return halves

    others = outer_forward(other_ref, rows, first_ref[1 - core])
    ((taps_real, taps_imag),) = forward(4)

    def with_taps(real, imag):
        return real * taps_real - imag * taps_imag, real * taps_imag + imag * taps_real

    def against_taps(real, imag):
        return real * taps_real + imag * taps_imag, imag * taps_real - real * taps_imag

    pairs = [forward(0, 1), forward(2, 3)]
    spectra = []
    cross_real = cross_imag = 0.0
    for value, grad in pairs:
        spectra += back(with_taps(*value), against_taps(*grad))
        cross_real = cross_real + (grad[0] * value[0] + grad[1] * value[1])
        cross_imag = cross_imag + (grad[1] * value[0] - grad[0] * value[1])
    spectra += back((cross_real, cross_imag))
    high, low = split(jnp.concatenate(spectra, axis=1))
    final = dot(last, jnp.concatenate((high, low, high), axis=0))

    def block(half, index):
        return final[half * CHIPS : (half + 1) * CHIPS, index * ROWS : (index + 1) * ROWS]

    results = []
    for slot in range(0, GROUP_SLOT, 2):
        results.append(block(0, slot) + block(1, slot + 1))
        results.append(block(0, slot + 1) - block(1, slot))
    results.append(block(0, GROUP_SLOT) + block(1, GROUP_SLOT + 1))
    scales = [scale_of(result, axis=1) for result in results]
    for slot, result in enumerate(results):
        rows[chip_rows(slot), :] = encode(result, scales[slot])
    rows[chip_rows(SCALE_SLOT), :] = join_scales(
        [jnp.broadcast_to(scale, (CHIPS, ROWS)) for scale in scales]
    )
    out_ref[...] = rows[...].astype(BF16)


def finish_kernel(
    in_ref,
    query_ref,
    key_ref,
    value_ref,
    upstream_ref,
    mixed_ref,
    gquery_ref,
    gkey_ref,
    gvalue_ref,
    gfilter_ref,
    turned,
    rows,
):
    rows[...] = in_ref[...].astype(F32)
    scales = rows[chip_rows(SCALE_SLOT), :]

    def collect(array):
        for owned in range(OWNED):
            slot = slot_of(array, owned)
            values = decode(rows[chip_rows(slot), :], scale_at(scales, slot))
            for sub in range(SUBS):
                turned[array, pl.ds(SUBS * owned + sub, GROUPS, stride=GROUPS), :] = values[
                    GROUPS * sub : GROUPS * (sub + 1)
                ]
        return jnp.transpose(turned[array])

    shares = decode(rows[chip_rows(GROUP_SLOT), :], scale_at(scales, GROUP_SLOT))
    parts = [shares[GROUPS * sub : GROUPS * (sub + 1)] for sub in range(SUBS)]
    gfilter_ref[...] = (parts[0] + parts[1]) + (parts[2] + parts[3])
    causal = collect(0)
    back_conv = collect(1)
    mixed_ref[...] = (query_ref[...].astype(F32) * causal).astype(BF16)
    gquery_ref[...] = (upstream_ref[...].astype(F32) * causal).astype(BF16)
    gkey_ref[...] = (back_conv * value_ref[...].astype(F32)).astype(BF16)
    gvalue_ref[...] = (back_conv * key_ref[...].astype(F32)).astype(BF16)


def swap_cores(values):
    count = lax.axis_size("inner")
    return lax.ppermute(values, "inner", [(i, i ^ 1) for i in range(count)])


def exchange(blocks):
    groups = [list(range(core, PIECES, 2)) for core in range(2)]
    return lax.all_to_all(
        blocks.reshape(CHIPS * SLOTS // 2, 2, ROWS),
        AXES,
        split_axis=0,
        concat_axis=0,
        tiled=True,
        axis_index_groups=groups,
    ).reshape(CHIPS * SLOTS, ROWS)


def per_device(gate_query, gate_key, value_input, filter_taps, grad_output):
    core = (lax.axis_index("inner") % 2).astype(jnp.int32).reshape(1)
    scalar = pl.BlockSpec(memory_space=pltpu.SMEM)
    whole = pl.BlockSpec(memory_space=pltpu.VMEM)
    small = pltpu.CompilerParams(vmem_limit_bytes=SMALL)
    packed = jax.ShapeDtypeStruct((CHIPS * SLOTS, ROWS), BF16)
    rows = pltpu.VMEM((CHIPS * SLOTS, ROWS), F32)
    turned = pltpu.VMEM((2, CHANNELS, ROWS), F32)
    far = pl.BlockSpec(memory_space=pltpu.HBM)
    wide = pltpu.VMEM((ROWS, CHANNELS), BF16)
    sources = (gate_query, gate_key, value_input, filter_taps, grad_output)
    blocks = pl.pallas_call(
        pack_kernel,
        out_shape=packed,
        in_specs=[far] * 5,
        out_specs=whole,
        scratch_shapes=[
            wide,
            wide,
            wide,
            pltpu.VMEM((GROUPS, ROWS), BF16),
            wide,
            turned,
            turned,
            rows,
            pltpu.SemaphoreType.DMA((5,)),
        ],
        compiler_params=small,
    )(*(pltpu.with_memory_space_constraint(source, pltpu.HBM) for source in sources))
    received = exchange(blocks)
    other = swap_cores(received)
    first, second, twist, last = (jnp.asarray(table) for table in tables())
    own = pl.pallas_call(
        own_kernel,
        out_shape=jax.ShapeDtypeStruct((PIECES, SLOTS * ROWS), F32),
        in_specs=[scalar, whole, whole],
        out_specs=whole,
        scratch_shapes=[rows],
        compiler_params=pltpu.CompilerParams(vmem_limit_bytes=LARGE),
    )(core, received, first)
    results = pl.pallas_call(
        convolve_kernel,
        out_shape=packed,
        in_specs=[scalar] + [whole] * 6,
        out_specs=whole,
        scratch_shapes=[rows],
        compiler_params=pltpu.CompilerParams(vmem_limit_bytes=LARGE),
    )(core, other, own, first, second, twist, last)
    out = jax.ShapeDtypeStruct((ROWS, CHANNELS), BF16)
    return pl.pallas_call(
        finish_kernel,
        out_shape=(out, out, out, out, jax.ShapeDtypeStruct((GROUPS, ROWS), F32)),
        in_specs=[whole] * 5,
        out_specs=(whole,) * 5,
        scratch_shapes=[turned, rows],
        compiler_params=small,
    )(exchange(results), gate_query, gate_key, value_input, grad_output)


def solution(mesh):
    rows = P(AXES, "chan")
    taps = P("chan", AXES)
    return jax.shard_map(
        per_device,
        mesh=mesh,
        in_specs=(rows, rows, rows, taps, rows),
        out_specs=(rows, rows, rows, rows, taps),
        check_vma=False,
    )
```

```python
import math

import jax
import jax.numpy as jnp
import numpy as np
from jax import lax
from jax.experimental import pallas as pl
from jax.experimental.pallas import tpu as pltpu
from jax.sharding import PartitionSpec as P

AXES = ("seq", "inner")
PIECES = 128
CHIPS = PIECES // 2
ROWS = 128
CHANNELS = 256
GROUPS = 16
SUBS = CHIPS // GROUPS
OWNED = 4
LENGTH = PIECES * ROWS
PADDED = 2 * LENGTH
OUTER = 2 * PIECES
GROUP_SLOT = 2 * OWNED
SCALE_SLOT = GROUP_SLOT + 1
SLOTS = SCALE_SLOT + 1
POWER = 64
RANGE = 125 / POWER
REACH = 2.0 ** (2 * RANGE) - 1.0
SHARE = 8
SMALL = 2 * 1024 * 1024
LARGE = 10 * 1024 * 1024
F32 = jnp.float32
BF16 = jnp.bfloat16


def split_table(table):
    high = table.astype(np.float32).astype(jnp.bfloat16)
    low = (table - high.astype(np.float64)).astype(jnp.bfloat16)
    return high, low


def tables():
    k1 = np.arange(OUTER)
    k1_half = np.arange(PIECES)
    t1 = np.stack((np.arange(0, PIECES, 2), np.arange(1, PIECES, 2)))
    t2 = np.arange(ROWS)
    outer = np.exp(-2j * np.pi * ((k1_half[None, :, None] * t1[:, None, :]) % OUTER) / OUTER)
    inner = np.exp(-2j * np.pi * ((t2[:, None] * t2[None, :]) % ROWS) / ROWS)
    twist = np.exp(-2j * np.pi * (k1[:, None] * t2[None, :]) / PADDED)
    first = np.concatenate((outer.real, outer.imag), axis=1)
    second = np.block([[inner.real, inner.imag], [-inner.imag, inner.real]])
    scale = 1.0 / (math.sqrt(LENGTH) * PADDED)
    last = np.swapaxes(np.concatenate((outer.real, outer.imag), axis=2), 1, 2) * scale
    first_high, first_low = split_table(first)
    second_high, second_low = split_table(second)
    last_high, last_low = split_table(last)
    return (
        np.concatenate((first_high, first_low, first_high), axis=2),
        np.concatenate((second_high, second_low), axis=0),
        np.stack((twist.real, twist.imag)).astype(np.float32),
        np.concatenate((last_high, last_low), axis=2),
    )


def split(values):
    high = values.astype(BF16)
    low = (values - high.astype(F32)).astype(BF16)
    return high, low


def dot(left, right):
    return jnp.dot(left, right, preferred_element_type=F32)


def scale_of(values, axis):
    peak = jnp.max(jnp.abs(values), axis=axis, keepdims=True)
    return (jnp.maximum(peak, 2.0**-118) * 1.0078125).astype(BF16).astype(F32)


def encode(values, scale):
    power = jnp.abs(values) * (REACH * 2.0**-RANGE / scale) + 2.0**-RANGE
    for _ in range(6):
        power = power * power
    return jnp.where(values < 0, -power, power)


def scale_at(scales, slot):
    return scales[:, SHARE * slot : SHARE * slot + 1]


def join_scales(scales):
    lane = lax.broadcasted_iota(jnp.int32, (scales[0].shape[0], ROWS), 1)
    joined = scales[0]
    for slot, scale in enumerate(scales[1:], 1):
        joined = jnp.where(lane < SHARE * slot, joined, scale)
    return joined


def decode(codes, scale):
    size = jnp.exp2(jnp.log2(jnp.abs(codes)) * (1.0 / POWER) + RANGE) - 1.0
    size = size * (scale * (1.0 / REACH))
    return jnp.where(codes < 0, -size, size)


def chip_rows(slot, first=0, count=CHIPS):
    return pl.ds(first * SLOTS + slot, count, stride=SLOTS)


def slot_of(array, owned):
    return 4 * (owned // 2) + 2 * array + owned % 2


def pack_kernel(
    query_ref, key_ref, value_ref, taps_ref, upstream_ref, out_ref, query, key, value, taps, upstream, turned, scaled, rows, sems
):
    moves = (
        (key_ref, key),
        (value_ref, value),
        (upstream_ref, upstream),
        (query_ref, query),
        (taps_ref, taps),
    )
    copies = [pltpu.make_async_copy(a, b, sems.at[i]) for i, (a, b) in enumerate(moves)]
    for copy in copies:
        copy.start()

    def place(array, left, right):
        product = left[...].astype(F32) * right[...].astype(F32)
        scale = scale_of(product, axis=0)
        codes = encode(product, scale).astype(BF16)
        turned[array] = jnp.transpose(codes).astype(F32)
        wide_scale = jnp.broadcast_to(scale.astype(BF16), (ROWS, CHANNELS))
        scaled[array] = jnp.transpose(wide_scale).astype(F32)
        for owned in range(OWNED):
            for sub in range(SUBS):
                rows[chip_rows(slot_of(array, owned), GROUPS * sub, GROUPS), :] = turned[
                    array, pl.ds(SUBS * owned + sub, GROUPS, stride=GROUPS), :
                ]

    for copy in copies:
        copy.wait()
    place(0, key, value)
    place(1, upstream, query)
    for sub in range(SUBS):
        rows[chip_rows(GROUP_SLOT, GROUPS * sub, GROUPS), :] = taps[...].astype(F32)
        scales = [None] * GROUP_SLOT
        for array in range(2):
            for owned in range(OWNED):
                scales[slot_of(array, owned)] = scaled[
                    array, pl.ds(SUBS * owned + sub, GROUPS, stride=GROUPS), :
                ]
        rows[chip_rows(SCALE_SLOT, GROUPS * sub, GROUPS), :] = join_scales(scales)
    out_ref[...] = rows[...].astype(BF16)


def outer_forward(in_ref, rows, table):
    rows[...] = in_ref[...].astype(F32)
    scales = rows[chip_rows(SCALE_SLOT), :]

    def transform(values):
        high, low = split(values)
        mixed = dot(table, jnp.concatenate((high, high, low), axis=0))
        return mixed[:PIECES], mixed[PIECES:]

    taps = transform(rows[chip_rows(GROUP_SLOT), :])
    results = []
    for first in range(0, GROUP_SLOT, 2):
        pair = [decode(rows[chip_rows(slot), :], scale_at(scales, slot)) for slot in (first, first + 1)]
        cosines, sines = transform(jnp.concatenate(pair, axis=1))
        results.append(
            (cosines[:, :ROWS] - sines[:, ROWS:], sines[:, :ROWS] + cosines[:, ROWS:])
        )
    return results + [taps]


def own_kernel(core_ref, in_ref, first_ref, out_ref, rows):
    for index, (real, imag) in enumerate(outer_forward(in_ref, rows, first_ref[core_ref[0]])):
        out_ref[:, 2 * index * ROWS : (2 * index + 1) * ROWS] = real
        out_ref[:, (2 * index + 1) * ROWS : (2 * index + 2) * ROWS] = imag


def convolve_kernel(core_ref, other_ref, own_ref, first_ref, second_ref, twist_ref, last_ref, out_ref, rows):
    core = core_ref[0]
    sign = (1 - 2 * core).astype(F32)
    second = jnp.concatenate(
        (second_ref[: 2 * ROWS], second_ref[: 2 * ROWS], second_ref[2 * ROWS :]), axis=0
    )
    table = last_ref[core]
    last = jnp.concatenate((table[:, :PIECES], table[:, :PIECES], table[:, PIECES:]), axis=1)
    twist_real, twist_imag = (
        jnp.concatenate((twist_ref[i, :PIECES], sign * twist_ref[i, PIECES:]), axis=0) for i in range(2)
    )

    def rotate(real, imag, way):
        return (
            real * twist_real - way * (imag * twist_imag),
            imag * twist_real + way * (real * twist_imag),
        )

    def inner(*sequences):
        whole = jnp.concatenate([jnp.concatenate(parts, axis=1) for parts in sequences], axis=0)
        high, low = split(whole)
        result = dot(jnp.concatenate((high, low, high), axis=1), second)
        return [
            (result[start : start + OUTER, :ROWS], result[start : start + OUTER, ROWS:])
            for start in range(0, len(sequences) * OUTER, OUTER)
        ]

    def both(index, part):
        column = (2 * index + part) * ROWS
        own, other = own_ref[:, column : column + ROWS], others[index][part]
        return jnp.concatenate((own + other, own - other), axis=0)

    def forward(*indices):
        return inner(*(rotate(both(index, 0), both(index, 1), 1.0) for index in indices))

    def back(*spectra):
        halves = []
        for turned_imag, turned_real in inner(*((imag, real) for real, imag in spectra)):
            turned = jnp.concatenate(rotate(turned_real, turned_imag, -1.0), axis=1)
            halves.append(turned[:PIECES] + turned[PIECES:])
        return halves

    others = outer_forward(other_ref, rows, first_ref[1 - core])
    ((taps_real, taps_imag),) = forward(4)

    def with_taps(real, imag):
        return real * taps_real - imag * taps_imag, real * taps_imag + imag * taps_real

    def against_taps(real, imag):
        return real * taps_real + imag * taps_imag, imag * taps_real - real * taps_imag

    pairs = [forward(0, 1), forward(2, 3)]
    spectra = []
    cross_real = cross_imag = 0.0
    for value, grad in pairs:
        spectra += back(with_taps(*value), against_taps(*grad))
        cross_real = cross_real + (grad[0] * value[0] + grad[1] * value[1])
        cross_imag = cross_imag + (grad[1] * value[0] - grad[0] * value[1])
    spectra += back((cross_real, cross_imag))
    high, low = split(jnp.concatenate(spectra, axis=1))
    final = dot(last, jnp.concatenate((high, low, high), axis=0))

    def block(half, index):
        return final[half * CHIPS : (half + 1) * CHIPS, index * ROWS : (index + 1) * ROWS]

    results = []
    for slot in range(0, GROUP_SLOT, 2):
        results.append(block(0, slot) + block(1, slot + 1))
        results.append(block(0, slot + 1) - block(1, slot))
    results.append(block(0, GROUP_SLOT) + block(1, GROUP_SLOT + 1))
    scales = [scale_of(result, axis=1) for result in results]
    for slot, result in enumerate(results):
        rows[chip_rows(slot), :] = encode(result, scales[slot])
    rows[chip_rows(SCALE_SLOT), :] = join_scales(
        [jnp.broadcast_to(scale, (CHIPS, ROWS)) for scale in scales]
    )
    out_ref[...] = rows[...].astype(BF16)


def finish_kernel(
    in_ref,
    query_ref,
    key_ref,
    value_ref,
    upstream_ref,
    mixed_ref,
    gquery_ref,
    gkey_ref,
    gvalue_ref,
    gfilter_ref,
    mixed,
    gquery,
    gkey,
    gvalue,
    gfilter,
    turned,
    rows,
    sems,
):
    rows[...] = in_ref[...].astype(F32)
    scales = rows[chip_rows(SCALE_SLOT), :]

    def collect(array):
        for owned in range(OWNED):
            slot = slot_of(array, owned)
            values = decode(rows[chip_rows(slot), :], scale_at(scales, slot))
            for sub in range(SUBS):
                turned[array, pl.ds(SUBS * owned + sub, GROUPS, stride=GROUPS), :] = values[
                    GROUPS * sub : GROUPS * (sub + 1)
                ]
        return jnp.transpose(turned[array])

    shares = decode(rows[chip_rows(GROUP_SLOT), :], scale_at(scales, GROUP_SLOT))
    parts = [shares[GROUPS * sub : GROUPS * (sub + 1)] for sub in range(SUBS)]
    gfilter[...] = (parts[0] + parts[1]) + (parts[2] + parts[3])
    causal = collect(0)
    back_conv = collect(1)
    mixed[...] = (query_ref[...].astype(F32) * causal).astype(BF16)
    gquery[...] = (upstream_ref[...].astype(F32) * causal).astype(BF16)
    gkey[...] = (back_conv * value_ref[...].astype(F32)).astype(BF16)
    gvalue[...] = (back_conv * key_ref[...].astype(F32)).astype(BF16)
    moves = (
        (mixed, mixed_ref),
        (gquery, gquery_ref),
        (gkey, gkey_ref),
        (gvalue, gvalue_ref),
        (gfilter, gfilter_ref),
    )
    copies = [pltpu.make_async_copy(a, b, sems.at[i]) for i, (a, b) in enumerate(moves)]
    for copy in copies:
        copy.start()
    for copy in copies:
        copy.wait()


def swap_cores(values):
    count = lax.axis_size("inner")
    return lax.ppermute(values, "inner", [(i, i ^ 1) for i in range(count)])


def exchange(blocks):
    groups = [list(range(core, PIECES, 2)) for core in range(2)]
    return lax.all_to_all(
        blocks.reshape(CHIPS * SLOTS // 2, 2, ROWS),
        AXES,
        split_axis=0,
        concat_axis=0,
        tiled=True,
        axis_index_groups=groups,
    ).reshape(CHIPS * SLOTS, ROWS)


def per_device(gate_query, gate_key, value_input, filter_taps, grad_output):
    core = (lax.axis_index("inner") % 2).astype(jnp.int32).reshape(1)
    scalar = pl.BlockSpec(memory_space=pltpu.SMEM)
    whole = pl.BlockSpec(memory_space=pltpu.VMEM)
    small = pltpu.CompilerParams(vmem_limit_bytes=SMALL)
    packed = jax.ShapeDtypeStruct((CHIPS * SLOTS, ROWS), BF16)
    rows = pltpu.VMEM((CHIPS * SLOTS, ROWS), F32)
    turned = pltpu.VMEM((2, CHANNELS, ROWS), F32)
    far = pl.BlockSpec(memory_space=pltpu.HBM)
    wide = pltpu.VMEM((ROWS, CHANNELS), BF16)
    sources = (gate_query, gate_key, value_input, filter_taps, grad_output)
    blocks = pl.pallas_call(
        pack_kernel,
        out_shape=packed,
        in_specs=[far] * 5,
        out_specs=whole,
        scratch_shapes=[
            wide,
            wide,
            wide,
            pltpu.VMEM((GROUPS, ROWS), BF16),
            wide,
            turned,
            turned,
            rows,
            pltpu.SemaphoreType.DMA((5,)),
        ],
        compiler_params=small,
    )(*(pltpu.with_memory_space_constraint(source, pltpu.HBM) for source in sources))
    received = exchange(blocks)
    other = swap_cores(received)
    first, second, twist, last = (jnp.asarray(table) for table in tables())
    own = pl.pallas_call(
        own_kernel,
        out_shape=jax.ShapeDtypeStruct((PIECES, SLOTS * ROWS), F32),
        in_specs=[scalar, whole, whole],
        out_specs=whole,
        scratch_shapes=[rows],
        compiler_params=pltpu.CompilerParams(vmem_limit_bytes=LARGE),
    )(core, received, first)
    results = pl.pallas_call(
        convolve_kernel,
        out_shape=packed,
        in_specs=[scalar] + [whole] * 6,
        out_specs=whole,
        scratch_shapes=[rows],
        compiler_params=pltpu.CompilerParams(vmem_limit_bytes=LARGE),
    )(core, other, own, first, second, twist, last)
    out = jax.ShapeDtypeStruct((ROWS, CHANNELS), BF16)
    return pl.pallas_call(
        finish_kernel,
        out_shape=(out, out, out, out, jax.ShapeDtypeStruct((GROUPS, ROWS), F32)),
        in_specs=[whole] * 5,
        out_specs=(far,) * 5,
        scratch_shapes=[
            wide,
            wide,
            wide,
            wide,
            pltpu.VMEM((GROUPS, ROWS), F32),
            turned,
            rows,
            pltpu.SemaphoreType.DMA((5,)),
        ],
        compiler_params=small,
    )(exchange(results), gate_query, gate_key, value_input, grad_output)


def solution(mesh):
    rows = P(AXES, "chan")
    taps = P("chan", AXES)
    return jax.shard_map(
        per_device,
        mesh=mesh,
        in_specs=(rows, rows, rows, taps, rows),
        out_specs=(rows, rows, rows, rows, taps),
        check_vma=False,
    )
```

```python
import math

import jax
import jax.numpy as jnp
import numpy as np
from jax import lax
from jax.experimental import pallas as pl
from jax.experimental.pallas import tpu as pltpu
from jax.sharding import PartitionSpec as P

AXES = ("seq", "inner")
PIECES = 128
CHIPS = PIECES // 2
ROWS = 128
CHANNELS = 256
GROUPS = 16
SUBS = CHIPS // GROUPS
OWNED = 4
LENGTH = PIECES * ROWS
PADDED = 2 * LENGTH
OUTER = 2 * PIECES
GROUP_SLOT = 2 * OWNED
SCALE_SLOT = GROUP_SLOT + 1
SLOTS = SCALE_SLOT + 1
POWER = 64
RANGE = 125 / POWER
REACH = 2.0 ** (2 * RANGE) - 1.0
SHARE = 8
SMALL = 2 * 1024 * 1024
LARGE = 10 * 1024 * 1024
F32 = jnp.float32
BF16 = jnp.bfloat16


def split_table(table):
    high = table.astype(np.float32).astype(jnp.bfloat16)
    low = (table - high.astype(np.float64)).astype(jnp.bfloat16)
    return high, low


def tables():
    k1 = np.arange(OUTER)
    k1_half = np.arange(PIECES)
    t1 = np.stack((np.arange(0, PIECES, 2), np.arange(1, PIECES, 2)))
    t2 = np.arange(ROWS)
    outer = np.exp(-2j * np.pi * ((k1_half[None, :, None] * t1[:, None, :]) % OUTER) / OUTER)
    inner = np.exp(-2j * np.pi * ((t2[:, None] * t2[None, :]) % ROWS) / ROWS)
    twist = np.exp(-2j * np.pi * (k1[:, None] * t2[None, :]) / PADDED)
    first = np.concatenate((outer.real, outer.imag), axis=1)
    second = np.block([[inner.real, inner.imag], [-inner.imag, inner.real]])
    scale = 1.0 / (math.sqrt(LENGTH) * PADDED)
    last = np.swapaxes(np.concatenate((outer.real, outer.imag), axis=2), 1, 2) * scale
    first_high, first_low = split_table(first)
    second_high, second_low = split_table(second)
    last_high, last_low = split_table(last)
    return (
        np.concatenate((first_high, first_low, first_high), axis=2),
        np.concatenate((second_high, second_low), axis=0),
        np.stack((twist.real, twist.imag)).astype(np.float32),
        np.concatenate((last_high, last_low), axis=2),
    )


def split(values):
    high = values.astype(BF16)
    low = (values - high.astype(F32)).astype(BF16)
    return high, low


def dot(left, right):
    return jnp.dot(left, right, preferred_element_type=F32)


def scale_of(values, axis):
    peak = jnp.max(jnp.abs(values), axis=axis, keepdims=True)
    return (jnp.maximum(peak, 2.0**-118) * 1.0078125).astype(BF16).astype(F32)


def encode(values, scale):
    power = jnp.abs(values) * (REACH * 2.0**-RANGE / scale) + 2.0**-RANGE
    for _ in range(6):
        power = power * power
    return jnp.where(values < 0, -power, power)


def scale_at(scales, slot):
    return scales[:, SHARE * slot : SHARE * slot + 1]


def join_scales(scales):
    lane = lax.broadcasted_iota(jnp.int32, (scales[0].shape[0], ROWS), 1)
    joined = scales[0]
    for slot, scale in enumerate(scales[1:], 1):
        joined = jnp.where(lane < SHARE * slot, joined, scale)
    return joined


def decode(codes, scale):
    size = jnp.exp2(jnp.log2(jnp.abs(codes)) * (1.0 / POWER) + RANGE) - 1.0
    size = size * (scale * (1.0 / REACH))
    return jnp.where(codes < 0, -size, size)


def chip_rows(slot, first=0, count=CHIPS):
    return pl.ds(first * SLOTS + slot, count, stride=SLOTS)


def slot_of(array, owned):
    return 4 * (owned // 2) + 2 * array + owned % 2


def pack_kernel(
    query_ref, key_ref, value_ref, taps_ref, upstream_ref, out_ref, query, key, value, taps, upstream, turned, scaled, rows, sems
):
    moves = (
        (key_ref, key),
        (value_ref, value),
        (upstream_ref, upstream),
        (query_ref, query),
        (taps_ref, taps),
    )
    copies = [pltpu.make_async_copy(a, b, sems.at[i]) for i, (a, b) in enumerate(moves)]
    for copy in copies:
        copy.start()

    def place(array, left, right):
        product = left[...].astype(F32) * right[...].astype(F32)
        scale = scale_of(product, axis=0)
        codes = encode(product, scale).astype(BF16)
        turned[array] = jnp.transpose(codes).astype(F32)
        wide_scale = jnp.broadcast_to(scale.astype(BF16), (ROWS, CHANNELS))
        scaled[array] = jnp.transpose(wide_scale).astype(F32)
        for owned in range(OWNED):
            for sub in range(SUBS):
                rows[chip_rows(slot_of(array, owned), GROUPS * sub, GROUPS), :] = turned[
                    array, pl.ds(SUBS * owned + sub, GROUPS, stride=GROUPS), :
                ]

    for copy in copies:
        copy.wait()
    place(0, key, value)
    place(1, upstream, query)
    for sub in range(SUBS):
        rows[chip_rows(GROUP_SLOT, GROUPS * sub, GROUPS), :] = taps[...].astype(F32)
        scales = [None] * GROUP_SLOT
        for array in range(2):
            for owned in range(OWNED):
                scales[slot_of(array, owned)] = scaled[
                    array, pl.ds(SUBS * owned + sub, GROUPS, stride=GROUPS), :
                ]
        rows[chip_rows(SCALE_SLOT, GROUPS * sub, GROUPS), :] = join_scales(scales)
    out_ref[...] = rows[...].astype(BF16)


def outer_forward(in_ref, rows, table):
    rows[...] = in_ref[...].astype(F32)
    scales = rows[chip_rows(SCALE_SLOT), :]

    def transform(values):
        high, low = split(values)
        mixed = dot(table, jnp.concatenate((high, high, low), axis=0))
        return mixed[:PIECES], mixed[PIECES:]

    taps = transform(rows[chip_rows(GROUP_SLOT), :])
    results = []
    for first in range(0, GROUP_SLOT, 2):
        pair = [decode(rows[chip_rows(slot), :], scale_at(scales, slot)) for slot in (first, first + 1)]
        cosines, sines = transform(jnp.concatenate(pair, axis=1))
        results.append(
            (cosines[:, :ROWS] - sines[:, ROWS:], sines[:, :ROWS] + cosines[:, ROWS:])
        )
    return results + [taps]


def own_kernel(core_ref, in_ref, first_ref, out_ref, rows):
    for index, (real, imag) in enumerate(outer_forward(in_ref, rows, first_ref[core_ref[0]])):
        out_ref[:, 2 * index * ROWS : (2 * index + 1) * ROWS] = real
        out_ref[:, (2 * index + 1) * ROWS : (2 * index + 2) * ROWS] = imag


def convolve_kernel(core_ref, other_ref, own_ref, first_ref, second_ref, twist_ref, last_ref, out_ref, rows):
    core = core_ref[0]
    sign = (1 - 2 * core).astype(F32)
    second = jnp.concatenate(
        (second_ref[: 2 * ROWS], second_ref[: 2 * ROWS], second_ref[2 * ROWS :]), axis=0
    )
    table = last_ref[core]
    last = jnp.concatenate((table[:, :PIECES], table[:, :PIECES], table[:, PIECES:]), axis=1)
    twist_real, twist_imag = (
        jnp.concatenate((twist_ref[i, :PIECES], sign * twist_ref[i, PIECES:]), axis=0) for i in range(2)
    )

    def rotate(real, imag, way):
        return (
            real * twist_real - way * (imag * twist_imag),
            imag * twist_real + way * (real * twist_imag),
        )

    def inner(*sequences):
        whole = jnp.concatenate([jnp.concatenate(parts, axis=1) for parts in sequences], axis=0)
        high, low = split(whole)
        result = dot(jnp.concatenate((high, low, high), axis=1), second)
        return [
            (result[start : start + OUTER, :ROWS], result[start : start + OUTER, ROWS:])
            for start in range(0, len(sequences) * OUTER, OUTER)
        ]

    def both(index, part):
        column = (2 * index + part) * ROWS
        own, other = own_ref[:, column : column + ROWS], others[index][part]
        return jnp.concatenate((own + other, own - other), axis=0)

    def forward(*indices):
        return inner(*(rotate(both(index, 0), both(index, 1), 1.0) for index in indices))

    def back(*spectra):
        halves = []
        for turned_imag, turned_real in inner(*((imag, real) for real, imag in spectra)):
            turned = jnp.concatenate(rotate(turned_real, turned_imag, -1.0), axis=1)
            halves.append(turned[:PIECES] + turned[PIECES:])
        return halves

    others = outer_forward(other_ref, rows, first_ref[1 - core])
    ((taps_real, taps_imag),) = forward(4)

    def with_taps(real, imag):
        return real * taps_real - imag * taps_imag, real * taps_imag + imag * taps_real

    def against_taps(real, imag):
        return real * taps_real + imag * taps_imag, imag * taps_real - real * taps_imag

    pairs = [forward(0, 1), forward(2, 3)]
    spectra = []
    cross_real = cross_imag = 0.0
    for value, grad in pairs:
        spectra += back(with_taps(*value), against_taps(*grad))
        cross_real = cross_real + (grad[0] * value[0] + grad[1] * value[1])
        cross_imag = cross_imag + (grad[1] * value[0] - grad[0] * value[1])
    spectra += back((cross_real, cross_imag))
    finals = []
    for spectrum in spectra:
        high, low = split(spectrum)
        finals.append(dot(last, jnp.concatenate((high, low, high), axis=0)))

    def block(half, index):
        column = index % 2 * ROWS
        return finals[index // 2][half * CHIPS : (half + 1) * CHIPS, column : column + ROWS]

    results = []
    for slot in range(0, GROUP_SLOT, 2):
        results.append(block(0, slot) + block(1, slot + 1))
        results.append(block(0, slot + 1) - block(1, slot))
    results.append(block(0, GROUP_SLOT) + block(1, GROUP_SLOT + 1))
    scales = [scale_of(result, axis=1) for result in results]
    for slot, result in enumerate(results):
        rows[chip_rows(slot), :] = encode(result, scales[slot])
    rows[chip_rows(SCALE_SLOT), :] = join_scales(
        [jnp.broadcast_to(scale, (CHIPS, ROWS)) for scale in scales]
    )
    out_ref[...] = rows[...].astype(BF16)


def finish_kernel(
    in_ref,
    query_ref,
    key_ref,
    value_ref,
    upstream_ref,
    mixed_ref,
    gquery_ref,
    gkey_ref,
    gvalue_ref,
    gfilter_ref,
    mixed,
    gquery,
    gkey,
    gvalue,
    gfilter,
    turned,
    rows,
    sems,
):
    rows[...] = in_ref[...].astype(F32)
    scales = rows[chip_rows(SCALE_SLOT), :]

    def collect(array):
        for owned in range(OWNED):
            slot = slot_of(array, owned)
            values = decode(rows[chip_rows(slot), :], scale_at(scales, slot))
            for sub in range(SUBS):
                turned[array, pl.ds(SUBS * owned + sub, GROUPS, stride=GROUPS), :] = values[
                    GROUPS * sub : GROUPS * (sub + 1)
                ]
        return jnp.transpose(turned[array])

    shares = decode(rows[chip_rows(GROUP_SLOT), :], scale_at(scales, GROUP_SLOT))
    parts = [shares[GROUPS * sub : GROUPS * (sub + 1)] for sub in range(SUBS)]
    gfilter[...] = (parts[0] + parts[1]) + (parts[2] + parts[3])
    causal = collect(0)
    back_conv = collect(1)
    mixed[...] = (query_ref[...].astype(F32) * causal).astype(BF16)
    gquery[...] = (upstream_ref[...].astype(F32) * causal).astype(BF16)
    gkey[...] = (back_conv * value_ref[...].astype(F32)).astype(BF16)
    gvalue[...] = (back_conv * key_ref[...].astype(F32)).astype(BF16)
    moves = (
        (mixed, mixed_ref),
        (gquery, gquery_ref),
        (gkey, gkey_ref),
        (gvalue, gvalue_ref),
        (gfilter, gfilter_ref),
    )
    copies = [pltpu.make_async_copy(a, b, sems.at[i]) for i, (a, b) in enumerate(moves)]
    for copy in copies:
        copy.start()
    for copy in copies:
        copy.wait()


def swap_cores(values):
    count = lax.axis_size("inner")
    return lax.ppermute(values, "inner", [(i, i ^ 1) for i in range(count)])


def exchange(blocks):
    groups = [list(range(core, PIECES, 2)) for core in range(2)]
    return lax.all_to_all(
        blocks.reshape(CHIPS * SLOTS // 2, 2, ROWS),
        AXES,
        split_axis=0,
        concat_axis=0,
        tiled=True,
        axis_index_groups=groups,
    ).reshape(CHIPS * SLOTS, ROWS)


def per_device(gate_query, gate_key, value_input, filter_taps, grad_output):
    core = (lax.axis_index("inner") % 2).astype(jnp.int32).reshape(1)
    scalar = pl.BlockSpec(memory_space=pltpu.SMEM)
    whole = pl.BlockSpec(memory_space=pltpu.VMEM)
    small = pltpu.CompilerParams(vmem_limit_bytes=SMALL)
    packed = jax.ShapeDtypeStruct((CHIPS * SLOTS, ROWS), BF16)
    rows = pltpu.VMEM((CHIPS * SLOTS, ROWS), F32)
    turned = pltpu.VMEM((2, CHANNELS, ROWS), F32)
    far = pl.BlockSpec(memory_space=pltpu.HBM)
    wide = pltpu.VMEM((ROWS, CHANNELS), BF16)
    sources = (gate_query, gate_key, value_input, filter_taps, grad_output)
    blocks = pl.pallas_call(
        pack_kernel,
        out_shape=packed,
        in_specs=[far] * 5,
        out_specs=whole,
        scratch_shapes=[
            wide,
            wide,
            wide,
            pltpu.VMEM((GROUPS, ROWS), BF16),
            wide,
            turned,
            turned,
            rows,
            pltpu.SemaphoreType.DMA((5,)),
        ],
        compiler_params=small,
    )(*(pltpu.with_memory_space_constraint(source, pltpu.HBM) for source in sources))
    received = exchange(blocks)
    other = swap_cores(received)
    first, second, twist, last = (jnp.asarray(table) for table in tables())
    own = pl.pallas_call(
        own_kernel,
        out_shape=jax.ShapeDtypeStruct((PIECES, SLOTS * ROWS), F32),
        in_specs=[scalar, whole, whole],
        out_specs=whole,
        scratch_shapes=[rows],
        compiler_params=pltpu.CompilerParams(vmem_limit_bytes=LARGE),
    )(core, received, first)
    results = pl.pallas_call(
        convolve_kernel,
        out_shape=packed,
        in_specs=[scalar] + [whole] * 6,
        out_specs=whole,
        scratch_shapes=[rows],
        compiler_params=pltpu.CompilerParams(vmem_limit_bytes=LARGE),
    )(core, other, own, first, second, twist, last)
    out = jax.ShapeDtypeStruct((ROWS, CHANNELS), BF16)
    return pl.pallas_call(
        finish_kernel,
        out_shape=(out, out, out, out, jax.ShapeDtypeStruct((GROUPS, ROWS), F32)),
        in_specs=[whole] * 5,
        out_specs=(far,) * 5,
        scratch_shapes=[
            wide,
            wide,
            wide,
            wide,
            pltpu.VMEM((GROUPS, ROWS), F32),
            turned,
            rows,
            pltpu.SemaphoreType.DMA((5,)),
        ],
        compiler_params=small,
    )(exchange(results), gate_query, gate_key, value_input, grad_output)


def solution(mesh):
    rows = P(AXES, "chan")
    taps = P("chan", AXES)
    return jax.shard_map(
        per_device,
        mesh=mesh,
        in_specs=(rows, rows, rows, taps, rows),
        out_specs=(rows, rows, rows, rows, taps),
        check_vma=False,
    )
```

```python
import math

import jax
import jax.numpy as jnp
import numpy as np
from jax import lax
from jax.experimental import pallas as pl
from jax.experimental.pallas import tpu as pltpu
from jax.sharding import PartitionSpec as P

AXES = ("seq", "inner")
PIECES = 128
CHIPS = PIECES // 2
ROWS = 128
CHANNELS = 256
GROUPS = 16
SUBS = CHIPS // GROUPS
OWNED = 4
LENGTH = PIECES * ROWS
PADDED = 2 * LENGTH
OUTER = 2 * PIECES
GROUP_SLOT = 2 * OWNED
SCALE_SLOT = GROUP_SLOT + 1
SLOTS = SCALE_SLOT + 1
POWER = 64
RANGE = 125 / POWER
REACH = 2.0 ** (2 * RANGE) - 1.0
SHARE = 8
SMALL = 2 * 1024 * 1024
LARGE = 10 * 1024 * 1024
F32 = jnp.float32
BF16 = jnp.bfloat16


def split_table(table):
    high = table.astype(np.float32).astype(jnp.bfloat16)
    low = (table - high.astype(np.float64)).astype(jnp.bfloat16)
    return high, low


def tables():
    k1 = np.arange(OUTER)
    k1_half = np.arange(PIECES)
    t1 = np.stack((np.arange(0, PIECES, 2), np.arange(1, PIECES, 2)))
    t2 = np.arange(ROWS)
    outer = np.exp(-2j * np.pi * ((k1_half[None, :, None] * t1[:, None, :]) % OUTER) / OUTER)
    inner = np.exp(-2j * np.pi * ((t2[:, None] * t2[None, :]) % ROWS) / ROWS)
    twist = np.exp(-2j * np.pi * (k1[:, None] * t2[None, :]) / PADDED)
    first = np.concatenate((outer.real, outer.imag), axis=1)
    second = np.block([[inner.real, inner.imag], [-inner.imag, inner.real]])
    scale = 1.0 / (math.sqrt(LENGTH) * PADDED)
    last = np.swapaxes(np.concatenate((outer.real, outer.imag), axis=2), 1, 2) * scale
    first_high, first_low = split_table(first)
    second_high, second_low = split_table(second)
    last_high, last_low = split_table(last)
    return (
        np.concatenate((first_high, first_low, first_high), axis=2),
        np.concatenate((second_high, second_low), axis=0),
        np.stack((twist.real, twist.imag)).astype(np.float32),
        np.concatenate((last_high, last_low), axis=2),
    )


def split(values):
    high = values.astype(BF16)
    low = (values - high.astype(F32)).astype(BF16)
    return high, low


def dot(left, right):
    return jnp.dot(left, right, preferred_element_type=F32)


def scale_of(values, axis):
    peak = jnp.max(jnp.abs(values), axis=axis, keepdims=True)
    return (jnp.maximum(peak, 2.0**-118) * 1.0078125).astype(BF16).astype(F32)


def encode(values, scale):
    power = jnp.abs(values) * (REACH * 2.0**-RANGE / scale) + 2.0**-RANGE
    for _ in range(6):
        power = power * power
    return jnp.where(values < 0, -power, power)


def scale_at(scales, slot):
    return scales[:, SHARE * slot : SHARE * slot + 1]


def join_scales(scales):
    lane = lax.broadcasted_iota(jnp.int32, (scales[0].shape[0], ROWS), 1)
    joined = scales[0]
    for slot, scale in enumerate(scales[1:], 1):
        joined = jnp.where(lane < SHARE * slot, joined, scale)
    return joined


def decode(codes, scale):
    size = jnp.exp2(jnp.log2(jnp.abs(codes)) * (1.0 / POWER) + RANGE) - 1.0
    size = size * (scale * (1.0 / REACH))
    return jnp.where(codes < 0, -size, size)


def chip_rows(slot, first=0, count=CHIPS):
    return pl.ds(first * SLOTS + slot, count, stride=SLOTS)


def slot_of(array, owned):
    return 4 * (owned // 2) + 2 * array + owned % 2


def pack_kernel(
    query_ref, key_ref, value_ref, taps_ref, upstream_ref, out_ref, query, key, value, taps, upstream, turned, scaled, rows, sems
):
    moves = (
        (key_ref, key),
        (value_ref, value),
        (upstream_ref, upstream),
        (query_ref, query),
        (taps_ref, taps),
    )
    copies = [pltpu.make_async_copy(a, b, sems.at[i]) for i, (a, b) in enumerate(moves)]
    for copy in copies:
        copy.start()

    def place(array, left, right):
        product = left[...].astype(F32) * right[...].astype(F32)
        scale = scale_of(product, axis=0)
        codes = encode(product, scale).astype(BF16)
        turned[array] = jnp.transpose(codes).astype(F32)
        wide_scale = jnp.broadcast_to(scale.astype(BF16), (ROWS, CHANNELS))
        scaled[array] = jnp.transpose(wide_scale).astype(F32)

    for copy in copies:
        copy.wait()
    place(0, key, value)
    place(1, upstream, query)
    for array in range(2):
        for owned in range(OWNED):
            for sub in range(SUBS):
                rows[chip_rows(slot_of(array, owned), GROUPS * sub, GROUPS), :] = turned[
                    array, pl.ds(SUBS * owned + sub, GROUPS, stride=GROUPS), :
                ]
    for sub in range(SUBS):
        rows[chip_rows(GROUP_SLOT, GROUPS * sub, GROUPS), :] = taps[...].astype(F32)
        scales = [None] * GROUP_SLOT
        for array in range(2):
            for owned in range(OWNED):
                scales[slot_of(array, owned)] = scaled[
                    array, pl.ds(SUBS * owned + sub, GROUPS, stride=GROUPS), :
                ]
        rows[chip_rows(SCALE_SLOT, GROUPS * sub, GROUPS), :] = join_scales(scales)
    out_ref[...] = rows[...].astype(BF16)


def outer_forward(in_ref, rows, table):
    rows[...] = in_ref[...].astype(F32)
    scales = rows[chip_rows(SCALE_SLOT), :]

    def transform(values):
        high, low = split(values)
        mixed = dot(table, jnp.concatenate((high, high, low), axis=0))
        return mixed[:PIECES], mixed[PIECES:]

    taps = transform(rows[chip_rows(GROUP_SLOT), :])
    results = []
    for first in range(0, GROUP_SLOT, 2):
        pair = [decode(rows[chip_rows(slot), :], scale_at(scales, slot)) for slot in (first, first + 1)]
        cosines, sines = transform(jnp.concatenate(pair, axis=1))
        results.append(
            (cosines[:, :ROWS] - sines[:, ROWS:], sines[:, :ROWS] + cosines[:, ROWS:])
        )
    return results + [taps]


def own_kernel(core_ref, in_ref, first_ref, out_ref, rows):
    for index, (real, imag) in enumerate(outer_forward(in_ref, rows, first_ref[core_ref[0]])):
        out_ref[:, 2 * index * ROWS : (2 * index + 1) * ROWS] = real
        out_ref[:, (2 * index + 1) * ROWS : (2 * index + 2) * ROWS] = imag


def convolve_kernel(core_ref, other_ref, own_ref, first_ref, second_ref, twist_ref, last_ref, out_ref, rows):
    core = core_ref[0]
    sign = (1 - 2 * core).astype(F32)
    second = jnp.concatenate(
        (second_ref[: 2 * ROWS], second_ref[: 2 * ROWS], second_ref[2 * ROWS :]), axis=0
    )
    table = last_ref[core]
    last = jnp.concatenate((table[:, :PIECES], table[:, :PIECES], table[:, PIECES:]), axis=1)
    twist_real, twist_imag = (
        jnp.concatenate((twist_ref[i, :PIECES], sign * twist_ref[i, PIECES:]), axis=0) for i in range(2)
    )

    def rotate(real, imag, way):
        return (
            real * twist_real - way * (imag * twist_imag),
            imag * twist_real + way * (real * twist_imag),
        )

    def inner(*sequences):
        whole = jnp.concatenate([jnp.concatenate(parts, axis=1) for parts in sequences], axis=0)
        high, low = split(whole)
        result = dot(jnp.concatenate((high, low, high), axis=1), second)
        return [
            (result[start : start + OUTER, :ROWS], result[start : start + OUTER, ROWS:])
            for start in range(0, len(sequences) * OUTER, OUTER)
        ]

    def both(index, part):
        column = (2 * index + part) * ROWS
        own, other = own_ref[:, column : column + ROWS], others[index][part]
        return jnp.concatenate((own + other, own - other), axis=0)

    def forward(*indices):
        return inner(*(rotate(both(index, 0), both(index, 1), 1.0) for index in indices))

    def back(*spectra):
        halves = []
        for turned_imag, turned_real in inner(*((imag, real) for real, imag in spectra)):
            turned = jnp.concatenate(rotate(turned_real, turned_imag, -1.0), axis=1)
            halves.append(turned[:PIECES] + turned[PIECES:])
        return halves

    others = outer_forward(other_ref, rows, first_ref[1 - core])
    ((taps_real, taps_imag),) = forward(4)

    def with_taps(real, imag):
        return real * taps_real - imag * taps_imag, real * taps_imag + imag * taps_real

    def against_taps(real, imag):
        return real * taps_real + imag * taps_imag, imag * taps_real - real * taps_imag

    pairs = [forward(0, 1), forward(2, 3)]
    spectra = []
    cross_real = cross_imag = 0.0
    for value, grad in pairs:
        spectra += back(with_taps(*value), against_taps(*grad))
        cross_real = cross_real + (grad[0] * value[0] + grad[1] * value[1])
        cross_imag = cross_imag + (grad[1] * value[0] - grad[0] * value[1])
    spectra += back((cross_real, cross_imag))
    finals = []
    for spectrum in spectra:
        high, low = split(spectrum)
        finals.append(dot(last, jnp.concatenate((high, low, high), axis=0)))

    def block(half, index):
        column = index % 2 * ROWS
        return finals[index // 2][half * CHIPS : (half + 1) * CHIPS, column : column + ROWS]

    results = []
    for slot in range(0, GROUP_SLOT, 2):
        results.append(block(0, slot) + block(1, slot + 1))
        results.append(block(0, slot + 1) - block(1, slot))
    results.append(block(0, GROUP_SLOT) + block(1, GROUP_SLOT + 1))
    scales = [scale_of(result, axis=1) for result in results]
    for slot, result in enumerate(results):
        rows[chip_rows(slot), :] = encode(result, scales[slot])
    rows[chip_rows(SCALE_SLOT), :] = join_scales(
        [jnp.broadcast_to(scale, (CHIPS, ROWS)) for scale in scales]
    )
    out_ref[...] = rows[...].astype(BF16)


def finish_kernel(
    in_ref,
    query_ref,
    key_ref,
    value_ref,
    upstream_ref,
    mixed_ref,
    gquery_ref,
    gkey_ref,
    gvalue_ref,
    gfilter_ref,
    mixed,
    gquery,
    gkey,
    gvalue,
    gfilter,
    turned,
    rows,
    sems,
):
    rows[...] = in_ref[...].astype(F32)
    scales = rows[chip_rows(SCALE_SLOT), :]

    def collect(array):
        for owned in range(OWNED):
            slot = slot_of(array, owned)
            values = decode(rows[chip_rows(slot), :], scale_at(scales, slot))
            for sub in range(SUBS):
                turned[array, pl.ds(SUBS * owned + sub, GROUPS, stride=GROUPS), :] = values[
                    GROUPS * sub : GROUPS * (sub + 1)
                ]
        return jnp.transpose(turned[array])

    shares = decode(rows[chip_rows(GROUP_SLOT), :], scale_at(scales, GROUP_SLOT))
    parts = [shares[GROUPS * sub : GROUPS * (sub + 1)] for sub in range(SUBS)]
    gfilter[...] = (parts[0] + parts[1]) + (parts[2] + parts[3])
    causal = collect(0)
    back_conv = collect(1)
    mixed[...] = (query_ref[...].astype(F32) * causal).astype(BF16)
    gquery[...] = (upstream_ref[...].astype(F32) * causal).astype(BF16)
    gkey[...] = (back_conv * value_ref[...].astype(F32)).astype(BF16)
    gvalue[...] = (back_conv * key_ref[...].astype(F32)).astype(BF16)
    moves = (
        (mixed, mixed_ref),
        (gquery, gquery_ref),
        (gkey, gkey_ref),
        (gvalue, gvalue_ref),
        (gfilter, gfilter_ref),
    )
    copies = [pltpu.make_async_copy(a, b, sems.at[i]) for i, (a, b) in enumerate(moves)]
    for copy in copies:
        copy.start()
    for copy in copies:
        copy.wait()


def swap_cores(values):
    count = lax.axis_size("inner")
    return lax.ppermute(values, "inner", [(i, i ^ 1) for i in range(count)])


def exchange(blocks):
    groups = [list(range(core, PIECES, 2)) for core in range(2)]
    return lax.all_to_all(
        blocks.reshape(CHIPS * SLOTS // 2, 2, ROWS),
        AXES,
        split_axis=0,
        concat_axis=0,
        tiled=True,
        axis_index_groups=groups,
    ).reshape(CHIPS * SLOTS, ROWS)


def per_device(gate_query, gate_key, value_input, filter_taps, grad_output):
    core = (lax.axis_index("inner") % 2).astype(jnp.int32).reshape(1)
    scalar = pl.BlockSpec(memory_space=pltpu.SMEM)
    whole = pl.BlockSpec(memory_space=pltpu.VMEM)
    small = pltpu.CompilerParams(vmem_limit_bytes=SMALL)
    packed = jax.ShapeDtypeStruct((CHIPS * SLOTS, ROWS), BF16)
    rows = pltpu.VMEM((CHIPS * SLOTS, ROWS), F32)
    turned = pltpu.VMEM((2, CHANNELS, ROWS), F32)
    far = pl.BlockSpec(memory_space=pltpu.HBM)
    wide = pltpu.VMEM((ROWS, CHANNELS), BF16)
    sources = (gate_query, gate_key, value_input, filter_taps, grad_output)
    blocks = pl.pallas_call(
        pack_kernel,
        out_shape=packed,
        in_specs=[far] * 5,
        out_specs=whole,
        scratch_shapes=[
            wide,
            wide,
            wide,
            pltpu.VMEM((GROUPS, ROWS), BF16),
            wide,
            turned,
            turned,
            rows,
            pltpu.SemaphoreType.DMA((5,)),
        ],
        compiler_params=small,
    )(*(pltpu.with_memory_space_constraint(source, pltpu.HBM) for source in sources))
    received = exchange(blocks)
    other = swap_cores(received)
    first, second, twist, last = (jnp.asarray(table) for table in tables())
    own = pl.pallas_call(
        own_kernel,
        out_shape=jax.ShapeDtypeStruct((PIECES, SLOTS * ROWS), F32),
        in_specs=[scalar, whole, whole],
        out_specs=whole,
        scratch_shapes=[rows],
        compiler_params=pltpu.CompilerParams(vmem_limit_bytes=LARGE),
    )(core, received, first)
    results = pl.pallas_call(
        convolve_kernel,
        out_shape=packed,
        in_specs=[scalar] + [whole] * 6,
        out_specs=whole,
        scratch_shapes=[rows],
        compiler_params=pltpu.CompilerParams(vmem_limit_bytes=LARGE),
    )(core, other, own, first, second, twist, last)
    out = jax.ShapeDtypeStruct((ROWS, CHANNELS), BF16)
    return pl.pallas_call(
        finish_kernel,
        out_shape=(out, out, out, out, jax.ShapeDtypeStruct((GROUPS, ROWS), F32)),
        in_specs=[whole] * 5,
        out_specs=(far,) * 5,
        scratch_shapes=[
            wide,
            wide,
            wide,
            wide,
            pltpu.VMEM((GROUPS, ROWS), F32),
            turned,
            rows,
            pltpu.SemaphoreType.DMA((5,)),
        ],
        compiler_params=small,
    )(exchange(results), gate_query, gate_key, value_input, grad_output)


def solution(mesh):
    rows = P(AXES, "chan")
    taps = P("chan", AXES)
    return jax.shard_map(
        per_device,
        mesh=mesh,
        in_specs=(rows, rows, rows, taps, rows),
        out_specs=(rows, rows, rows, rows, taps),
        check_vma=False,
    )
```
